32 devices in a mesh: stream: 8 (over y, x, core), azim: 4 (over z).
Axes of the slice: x: 2, y: 2, z: 4, core: 2. Of those that a mesh axis runs over, the one named last changes fastest.
Arguments:
- start_vector: bfloat16 [32, 4, 8, 64, 128], P('stream', 'azim'), may hold values from -6 to 6
- trace_blocks: bfloat16 [32, 4, 8, 64, 768], P('stream', 'azim'), may hold values from -0.21875 to 0.21875
- neighbour: int32 [4, 8, 12], P('azim'), may hold values from 0 to 71
Outputs:
- krylov_basis: bfloat16 [4, 32, 4, 8, 64, 128], P(None, 'stream', 'azim')
The draws below stay inside these ranges and needn't reach their ends.
Inputs may be any that keep to these rules, and one draw needn't show every extreme that they name: `neighbour`: entry e names column offsets (e // 24 - 1, (e // 8) % 3 - 1) and slot e % 8; the list is the same for every stream column.
All inputs are finite; a program needn't handle non-finite values.
Results may differ from the reference program's by a relative error of at most 0.0055.
Values may be sent and summed in bfloat16 or wider, within the bound.
No kernel may reach another device: no remote copies, remote signals or barrier semaphores. Data moves between devices by JAX's collectives and lax.ppermute only.
A program may use at most 64 MiB of HBM per device.

```python
import jax
import jax.numpy as jnp
from jax import lax

FB = 64
NB = 12
STEPS = 4
C = 8
R = 128
NS = 32
NA = 4


def place_ends(drawn, own_key, low, top_value):
    longest = drawn.shape.index(max(drawn.shape))
    spots = []
    for shift in (0, 1):
        where = [jax.random.randint(jax.random.fold_in(own_key, axis), (), 0, length) for axis, length in enumerate(drawn.shape)]
        where[longest] = (where[longest] + shift) % drawn.shape[longest]
        spots.append(tuple(where))
    return drawn.at[spots[0]].set(low).at[spots[1]].set(top_value)


def shard_levels(own_key, dims, split, least, high):
    def one(dim, parts):
        draws = jax.random.uniform(jax.random.fold_in(jax.random.fold_in(own_key, 6), dim), (parts,), jnp.float32, least / len(split), high / len(split))
        return jnp.repeat(jnp.exp(draws), dims[dim] // parts).reshape((-1,) + (1,) * (len(dims) - dim - 1))

    level = one(*split[0])
    for cut in split[1:]:
        level = level * one(*cut)
    return level


def scatter_about(key, dims, deviation, bound, pieces=(), held_as=jnp.bfloat16):
    entries = jax.random.normal(key, dims, jnp.float32) * deviation
    if len(pieces) > 0:
        entries = shard_levels(key, dims, pieces, -0.22, 0.18) * entries
    return jnp.clip(entries, min=-bound, max=bound).astype(held_as)


def setup_inputs(seed: int = 0) -> dict:
    key_list = jax.random.split(jax.random.key(seed), 4)
    return {
        "start_vector": scatter_about(key_list[0], (NS, NA, C, FB, R), 1.0, 6.0, ((0, 8), (1, 4))),
        "trace_blocks": scatter_about(key_list[1], (NS, NA, C, FB, NB * FB), (NB * FB) ** -0.5, 0.21875, ((0, 8), (1, 4))),
        "neighbour": place_ends(jax.random.randint(key_list[2], (NA, C, NB), 0, 9 * C), jax.random.fold_in(key_list[2], 1), 0, (9 * C) - 1).astype(jnp.int32),
    }


def apply_rows(padded, blocks, neighbour, rows):
    column_count = padded.shape[1] - 2
    face_count = padded.shape[2]
    offset_code = neighbour // face_count
    slot_index = neighbour - offset_code * face_count
    stream_shift = offset_code // 3
    azim_shift = offset_code - stream_shift * 3
    row_index = jnp.arange(rows, dtype=jnp.int32)[:, None, None, None]
    column_index = jnp.arange(column_count, dtype=jnp.int32)[None, :, None, None]
    gathered = padded[row_index + stream_shift[None], column_index + azim_shift[None], slot_index[None]]
    gathered = gathered.reshape(rows, column_count, face_count, -1, padded.shape[-1])
    product = jnp.einsum("ijcam,ijcmr->ijcar", blocks.astype(jnp.float32), gathered.astype(jnp.float32))
    return product.astype(jnp.bfloat16)


def reference(start_vector, trace_blocks, neighbour):
    current = start_vector
    basis = []
    for layer_index in range(STEPS):
        wrapped = jnp.concatenate([current[-1:], current, current[:1]], axis=0)
        wrapped = jnp.concatenate([wrapped[:, -1:], wrapped, wrapped[:, :1]], axis=1)

        def one_column(position):
            window = lax.dynamic_slice_in_dim(wrapped, position, 3, 0)
            blocks = lax.dynamic_slice_in_dim(trace_blocks, position, 1, 0)
            return apply_rows(window, blocks, neighbour, 1)[0]

        current = lax.map(one_column, jnp.arange(NS, dtype=jnp.int32))
        basis.append(current)
    return jnp.stack(basis)
```

```python
import functools

import jax
import jax.numpy as jnp
from jax import lax
from jax.experimental import pallas as pl
from jax.experimental.pallas import tpu as pltpu
from jax.sharding import PartitionSpec as P

STEPS = 4
HALVES = 2
VMEM_LIMIT = 24 * 1024 * 1024


def low_lanes(shape):
    return lax.broadcasted_iota(jnp.int32, shape, len(shape) - 1) < shape[-1] // 2


def swap_lanes(value):
    return pltpu.roll(value, value.shape[-1] // 2, len(value.shape) - 1)


def pack_kernel(start_ref, first_ref, second_ref):
    faces, width, lanes = start_ref.shape[1:]
    for face in range(faces):
        value = start_ref[0, face].astype(jnp.float32)
        top = value[: width // 2]
        bottom = swap_lanes(value[width // 2 :])
        low = low_lanes(top.shape)
        first_ref[0, face] = jnp.where(low, top, bottom).astype(jnp.bfloat16)
        second_ref[0, face] = jnp.where(low, bottom, top).astype(jnp.bfloat16)


def pack(start):
    columns, faces, width, lanes = start.shape
    half = jax.ShapeDtypeStruct((columns, faces, width // 2, lanes), jnp.bfloat16)
    spec = pl.BlockSpec((1, faces, width // 2, lanes), lambda i: (i, 0, 0, 0))
    return pl.pallas_call(
        pack_kernel,
        grid=(columns,),
        in_specs=[pl.BlockSpec((1, faces, width, lanes), lambda i: (i, 0, 0, 0))],
        out_specs=[spec, spec],
        out_shape=[half, half],
        name="pack",
    )(start)


def step_kernel(half, with_basis, *refs):
    (table, blocks_ref, own, low_az, high_az, low_st, high_st), refs = refs[:7], refs[7:]
    if with_basis:
        other_ref, refs = refs[0], refs[1:]
        if len(refs) == 5:
            refs = refs[1:]
        next_ref, basis_ref, window, sems = refs
    else:
        next_ref, window, sems = refs
    faces, width, depth = blocks_ref.shape[1:]
    columns = own.shape[0]
    span = columns + 2
    rows, lanes = window.shape[1:]
    i = pl.program_id(0)

    @pl.when(i == 0)
    def _():
        copies = []
        view = window.reshape(3, span, faces, rows, lanes)
        for azim, source in enumerate((low_az, own, high_az)):
            copies.append((source, view.at[azim, pl.ds(1, columns)]))
        for azim in range(3):
            copies.append((low_st.at[azim], view.at[azim, 0]))
            copies.append((high_st.at[azim], view.at[azim, span - 1]))
        started = [
            pltpu.make_async_copy(source, target, sems.at[n])
            for n, (source, target) in enumerate(copies)
        ]
        for copy in started:
            copy.start()
        for copy in started:
            copy.wait()

    neighbours = table.shape[1]
    low = low_lanes((rows, lanes))
    for face in range(faces):
        gathered = jnp.concatenate(
            [window[table[face, k] + i * faces] for k in range(neighbours)], axis=0
        )
        block = blocks_ref[0, face]
        stacked = jnp.concatenate([block[:, : depth // 2], block[:, depth // 2 :]], axis=0)
        product = jnp.dot(stacked, gathered, preferred_element_type=jnp.float32)
        top, bottom = product[:width], product[width:]
        if half == 0:
            here = jnp.where(low, top[:rows], bottom[rows:])
            there = jnp.where(low, top[rows:], bottom[:rows])
        else:
            here = jnp.where(low, bottom[rows:], top[:rows])
            there = jnp.where(low, bottom[:rows], top[rows:])
        result = (here + swap_lanes(there)).astype(jnp.bfloat16)
        next_ref[0, face] = result
        if with_basis:
            second = result.astype(jnp.float32)
            first = other_ref[0, face].astype(jnp.float32)
            basis_ref[0, 0, face, :rows] = jnp.where(low, first, second).astype(jnp.bfloat16)
            basis_ref[0, 0, face, rows:] = swap_lanes(jnp.where(low, second, first)).astype(
                jnp.bfloat16
            )


def step(half, index, table, blocks, pieces, other=None, basis=None):
    columns, faces, width, depth = blocks.shape
    rows, lanes = pieces[0].shape[2:]
    with_basis = half == HALVES - 1
    piece_spec = pl.BlockSpec((1, faces, rows, lanes), lambda i: (i, 0, 0, 0))
    any_spec = pl.BlockSpec(memory_space=pl.ANY)
    in_specs = [
        pl.BlockSpec(memory_space=pltpu.SMEM),
        pl.BlockSpec((1, faces, width, depth), lambda i: (i, 0, 0, 0)),
    ] + [any_spec] * 5
    args = [table, blocks, *pieces]
    out_specs = [piece_spec]
    out_shape = [jax.ShapeDtypeStruct((columns, faces, rows, lanes), jnp.bfloat16)]
    aliases = {}
    if with_basis:
        in_specs.append(piece_spec)
        args.append(other)
        if basis is not None:
            in_specs.append(any_spec)
            aliases = {len(args): 1}
            args.append(basis)
        out_specs.append(
            pl.BlockSpec((1, 1, faces, width, lanes), lambda i: (index, i, 0, 0, 0))
        )
        out_shape.append(jax.ShapeDtypeStruct((STEPS, columns, faces, width, lanes), jnp.bfloat16))
    flops = 2 * columns * faces * 2 * width * (depth // 2) * lanes
    return pl.pallas_call(
        functools.partial(step_kernel, half, with_basis),
        grid=(columns,),
        in_specs=in_specs,
        out_specs=out_specs,
        out_shape=out_shape,
        input_output_aliases=aliases,
        scratch_shapes=[
            pltpu.VMEM((3 * (columns + 2) * faces, rows, lanes), jnp.bfloat16),
            pltpu.SemaphoreType.DMA((9,)),
        ],
        cost_estimate=pl.CostEstimate(flops=flops, bytes_accessed=blocks.size * 2, transcendentals=0),
        compiler_params=pltpu.CompilerParams(vmem_limit_bytes=VMEM_LIMIT),
        name=f"step_half{half}",
    )(*args)


def shift(value, axis, up):
    count = lax.axis_size(axis)
    pairs = [(i, (i + 1) % count) for i in range(count)]
    if not up:
        pairs = [(target, source) for source, target in pairs]
    return lax.ppermute(value, axis, pairs)


def halves_of_rows(blocks):
    columns, faces, width, depth = blocks.shape
    row = lax.broadcasted_iota(jnp.int32, (depth, depth), 0)
    column = lax.broadcasted_iota(jnp.int32, (depth, depth), 1)
    part = width // 2
    place = (row // width) * part + row % part + ((row // part) % 2) * (depth // 2)
    mover = (place == column).astype(jnp.bfloat16)
    moved = jnp.dot(blocks.reshape(-1, depth), mover, preferred_element_type=jnp.float32)
    return moved.astype(jnp.bfloat16).reshape(blocks.shape)


def local(start_vector, trace_blocks, neighbour):
    columns, around, faces, width, lanes = start_vector.shape
    start = start_vector.reshape(columns, faces, width, lanes)
    blocks = halves_of_rows(trace_blocks.reshape(columns, faces, width, -1))
    codes = neighbour.reshape(faces, -1)
    table = (((codes // faces) % 3) * (columns + 2) + codes // (3 * faces)) * faces + codes % faces
    current = list(pack(start))
    basis = None
    for index in range(STEPS):
        around_z = [
            (shift(current[h], "azim", True), shift(current[h], "azim", False))
            for h in range(HALVES)
        ]
        for h in range(HALVES):
            low_az, high_az = around_z[h]
            trio = (low_az, current[h], high_az)
            low_st = shift(jnp.stack([part[columns - 1] for part in trio]), "stream", True)
            high_st = shift(jnp.stack([part[0] for part in trio]), "stream", False)
            pieces = (current[h], low_az, high_az, low_st, high_st)
            if h < HALVES - 1:
                (current[h],) = step(h, index, table, blocks, pieces)
            else:
                current[h], basis = step(
                    h, index, table, blocks, pieces, other=current[0], basis=basis
                )
    return basis.reshape(STEPS, columns, around, faces, width, lanes)


def solution(mesh):
    return jax.shard_map(
        local,
        mesh=mesh,
        in_specs=(
            P("stream", "azim", None, None, None),
            P("stream", "azim", None, None, None),
            P("azim", None, None),
        ),
        out_specs=P(None, "stream", "azim", None, None, None),
        check_vma=False,
    )
```

```python
import functools

import jax
import jax.numpy as jnp
from jax import lax
from jax.experimental import pallas as pl
from jax.experimental.pallas import tpu as pltpu
from jax.sharding import PartitionSpec as P

STEPS = 4
HALVES = 2
VMEM_LIMIT = 24 * 1024 * 1024


def low_lanes(shape):
    return lax.broadcasted_iota(jnp.int32, shape, len(shape) - 1) < shape[-1] // 2


def swap_lanes(value):
    return pltpu.roll(value, value.shape[-1] // 2, len(value.shape) - 1)


def pack_kernel(start_ref, first_ref, second_ref):
    faces, width, lanes = start_ref.shape[1:]
    for face in range(faces):
        value = start_ref[0, face].astype(jnp.float32)
        top = value[: width // 2]
        bottom = swap_lanes(value[width // 2 :])
        low = low_lanes(top.shape)
        first_ref[0, face] = jnp.where(low, top, bottom).astype(jnp.bfloat16)
        second_ref[0, face] = jnp.where(low, bottom, top).astype(jnp.bfloat16)


def pack(start):
    columns, faces, width, lanes = start.shape
    half = jax.ShapeDtypeStruct((columns, faces, width // 2, lanes), jnp.bfloat16)
    spec = pl.BlockSpec((1, faces, width // 2, lanes), lambda i: (i, 0, 0, 0))
    return pl.pallas_call(
        pack_kernel,
        grid=(columns,),
        in_specs=[pl.BlockSpec((1, faces, width, lanes), lambda i: (i, 0, 0, 0))],
        out_specs=[spec, spec],
        out_shape=[half, half],
        name="pack",
    )(start)


def step_kernel(half, with_basis, *refs):
    (table, blocks_ref, even_pair, odd_pair, low_st, high_st), refs = refs[:6], refs[6:]
    if with_basis:
        other_ref, refs = refs[0], refs[1:]
        if len(refs) == 5:
            refs = refs[1:]
        next_ref, basis_ref, window, sems = refs
    else:
        next_ref, window, sems = refs
    faces, width, depth = blocks_ref.shape[1:]
    columns = even_pair.shape[1]
    span = columns + 2
    rows, lanes = window.shape[1:]
    i = pl.program_id(0)

    @pl.when(i == 0)
    def _():
        copies = []
        view = window.reshape(4, span, faces, rows, lanes)
        for azim in range(4):
            source = (even_pair, odd_pair)[azim // 2].at[azim % 2]
            copies.append((source, view.at[azim, pl.ds(1, columns)]))
            copies.append((low_st.at[azim], view.at[azim, 0]))
            copies.append((high_st.at[azim], view.at[azim, span - 1]))
        started = [
            pltpu.make_async_copy(source, target, sems.at[n])
            for n, (source, target) in enumerate(copies)
        ]
        for copy in started:
            copy.start()
        for copy in started:
            copy.wait()

    neighbours = table.shape[1]
    low = low_lanes((rows, lanes))
    for face in range(faces):
        gathered = jnp.concatenate(
            [window[table[face, k] + i * faces] for k in range(neighbours)], axis=0
        )
        block = blocks_ref[0, face]
        stacked = jnp.concatenate([block[:, : depth // 2], block[:, depth // 2 :]], axis=0)
        product = jnp.dot(stacked, gathered, preferred_element_type=jnp.float32)
        top, bottom = product[:width], product[width:]
        if half == 0:
            here = jnp.where(low, top[:rows], bottom[rows:])
            there = jnp.where(low, top[rows:], bottom[:rows])
        else:
            here = jnp.where(low, bottom[rows:], top[:rows])
            there = jnp.where(low, bottom[:rows], top[rows:])
        result = (here + swap_lanes(there)).astype(jnp.bfloat16)
        next_ref[0, face] = result
        if with_basis:
            second = result.astype(jnp.float32)
            first = other_ref[0, face].astype(jnp.float32)
            basis_ref[0, 0, face, :rows] = jnp.where(low, first, second).astype(jnp.bfloat16)
            basis_ref[0, 0, face, rows:] = swap_lanes(jnp.where(low, second, first)).astype(
                jnp.bfloat16
            )


def step(half, index, table, blocks, pieces, other=None, basis=None):
    columns, faces, width, depth = blocks.shape
    rows, lanes = pieces[0].shape[3:]
    with_basis = half == HALVES - 1
    piece_spec = pl.BlockSpec((1, faces, rows, lanes), lambda i: (i, 0, 0, 0))
    any_spec = pl.BlockSpec(memory_space=pl.ANY)
    in_specs = [
        pl.BlockSpec(memory_space=pltpu.SMEM),
        pl.BlockSpec((1, faces, width, depth), lambda i: (i, 0, 0, 0)),
    ] + [any_spec] * 4
    args = [table, blocks, *pieces]
    out_specs = [piece_spec]
    out_shape = [jax.ShapeDtypeStruct((columns, faces, rows, lanes), jnp.bfloat16)]
    aliases = {}
    if with_basis:
        in_specs.append(piece_spec)
        args.append(other)
        if basis is not None:
            in_specs.append(any_spec)
            aliases = {len(args): 1}
            args.append(basis)
        out_specs.append(
            pl.BlockSpec((1, 1, faces, width, lanes), lambda i: (index, i, 0, 0, 0))
        )
        out_shape.append(jax.ShapeDtypeStruct((STEPS, columns, faces, width, lanes), jnp.bfloat16))
    flops = 2 * columns * faces * 2 * width * (depth // 2) * lanes
    return pl.pallas_call(
        functools.partial(step_kernel, half, with_basis),
        grid=(columns,),
        in_specs=in_specs,
        out_specs=out_specs,
        out_shape=out_shape,
        input_output_aliases=aliases,
        scratch_shapes=[
            pltpu.VMEM((4 * (columns + 2) * faces, rows, lanes), jnp.bfloat16),
            pltpu.SemaphoreType.DMA((12,)),
        ],
        cost_estimate=pl.CostEstimate(flops=flops, bytes_accessed=blocks.size * 2, transcendentals=0),
        compiler_params=pltpu.CompilerParams(vmem_limit_bytes=VMEM_LIMIT),
        name=f"step_half{half}",
    )(*args)


def shift(value, axis, up):
    count = lax.axis_size(axis)
    pairs = [(i, (i + 1) % count) for i in range(count)]
    if not up:
        pairs = [(target, source) for source, target in pairs]
    return lax.ppermute(value, axis, pairs)


def with_partner(value, offset):
    count = lax.axis_size("azim")
    groups = [[i + offset, (i + offset + 1) % count] for i in range(0, count, 2)]
    return lax.all_gather(value, "azim", axis_index_groups=groups)


def halves_of_rows(blocks):
    columns, faces, width, depth = blocks.shape
    row = lax.broadcasted_iota(jnp.int32, (depth, depth), 0)
    column = lax.broadcasted_iota(jnp.int32, (depth, depth), 1)
    part = width // 2
    place = (row // width) * part + row % part + ((row // part) % 2) * (depth // 2)
    mover = (place == column).astype(jnp.bfloat16)
    moved = jnp.dot(blocks.reshape(-1, depth), mover, preferred_element_type=jnp.float32)
    return moved.astype(jnp.bfloat16).reshape(blocks.shape)


def local(start_vector, trace_blocks, neighbour):
    columns, around, faces, width, lanes = start_vector.shape
    start = start_vector.reshape(columns, faces, width, lanes)
    blocks = halves_of_rows(trace_blocks.reshape(columns, faces, width, -1))
    codes = neighbour.reshape(faces, -1)
    place = jnp.where(lax.axis_index("azim") % 2 == 0, jnp.array([2, 0, 1]), jnp.array([0, 1, 3]))
    table = (place[(codes // faces) % 3] * (columns + 2) + codes // (3 * faces)) * faces + codes % faces
    current = list(pack(start))
    basis = None
    for index in range(STEPS):
        around_z = [
            (with_partner(current[h], 0), with_partner(current[h], 1))
            for h in range(HALVES)
        ]
        for h in range(HALVES):
            pairs = around_z[h]
            low_st = shift(
                jnp.concatenate([pair[:, columns - 1] for pair in pairs]), "stream", True
            )
            high_st = shift(jnp.concatenate([pair[:, 0] for pair in pairs]), "stream", False)
            pieces = (*pairs, low_st, high_st)
            if h < HALVES - 1:
                (current[h],) = step(h, index, table, blocks, pieces)
            else:
                current[h], basis = step(
                    h, index, table, blocks, pieces, other=current[0], basis=basis
                )
    return basis.reshape(STEPS, columns, around, faces, width, lanes)


def solution(mesh):
    return jax.shard_map(
        local,
        mesh=mesh,
        in_specs=(
            P("stream", "azim", None, None, None),
            P("stream", "azim", None, None, None),
            P("azim", None, None),
        ),
        out_specs=P(None, "stream", "azim", None, None, None),
        check_vma=False,
    )
```

```python
import functools

import jax
import jax.numpy as jnp
from jax import lax
from jax.experimental import pallas as pl
from jax.experimental.pallas import tpu as pltpu
from jax.sharding import PartitionSpec as P

STEPS = 4
HALVES = 2
VMEM_LIMIT = 24 * 1024 * 1024
ANY = pl.BlockSpec(memory_space=pl.ANY)


def low_lanes(shape):
    return lax.broadcasted_iota(jnp.int32, shape, len(shape) - 1) < shape[-1] // 2


def swap_lanes(value):
    return pltpu.roll(value, value.shape[-1] // 2, len(value.shape) - 1)


def pack_kernel(start_ref, first_ref, second_ref):
    faces, width, lanes = start_ref.shape[1:]
    for face in range(faces):
        value = start_ref[0, face].astype(jnp.float32)
        top = value[: width // 2]
        bottom = swap_lanes(value[width // 2 :])
        low = low_lanes(top.shape)
        first_ref[0, face] = jnp.where(low, top, bottom).astype(jnp.bfloat16)
        second_ref[0, face] = jnp.where(low, bottom, top).astype(jnp.bfloat16)


def pack(start):
    columns, faces, width, lanes = start.shape
    half = jax.ShapeDtypeStruct((columns, faces, width // 2, lanes), jnp.bfloat16)
    spec = pl.BlockSpec((1, faces, width // 2, lanes), lambda i: (i, 0, 0, 0))
    return pl.pallas_call(
        pack_kernel,
        grid=(columns,),
        in_specs=[pl.BlockSpec((1, faces, width, lanes), lambda i: (i, 0, 0, 0))],
        out_specs=[spec, spec],
        out_shape=[half, half],
        name="pack",
    )(start)


def unpacked(first, second):
    first = first.astype(jnp.float32)
    second = second.astype(jnp.float32)
    low = low_lanes(first.shape)
    top = jnp.where(low, first, second).astype(jnp.bfloat16)
    bottom = swap_lanes(jnp.where(low, second, first)).astype(jnp.bfloat16)
    return top, bottom


def unpack_kernel(first_ref, second_ref, *refs):
    basis_ref = refs[-1]
    faces, rows = first_ref.shape[1:3]
    for face in range(faces):
        top, bottom = unpacked(first_ref[0, face], second_ref[0, face])
        basis_ref[0, 0, face, :rows] = top
        basis_ref[0, 0, face, rows:] = bottom


def unpack(index, first, second, basis):
    columns, faces, rows, lanes = first.shape
    spec = pl.BlockSpec((1, faces, rows, lanes), lambda i: (i, 0, 0, 0))
    return pl.pallas_call(
        unpack_kernel,
        grid=(columns,),
        in_specs=[spec, spec] + ([] if basis is None else [ANY]),
        out_specs=pl.BlockSpec(
            (1, 1, faces, 2 * rows, lanes), lambda i: (index, i, 0, 0, 0)
        ),
        out_shape=jax.ShapeDtypeStruct((STEPS, columns, faces, 2 * rows, lanes), jnp.bfloat16),
        input_output_aliases={} if basis is None else {2: 0},
        name="unpack",
    )(first, second, *([] if basis is None else [basis]))


def run_copies(copies):
    for copy in copies:
        copy.start()
    for copy in copies:
        copy.wait()


def edges_kernel(own, low_az, high_az, after, to_low, to_high, sems):
    columns = own.shape[0]
    copies = []
    for azim, source in enumerate((low_az, own, high_az)):
        copies.append((source.at[0], to_low.at[azim]))
        copies.append((source.at[columns - 1], to_high.at[azim]))
    run_copies(
        [
            pltpu.make_async_copy(source, target, sems.at[n])
            for n, (source, target) in enumerate(copies)
        ]
    )


def edges(own, low_az, high_az, after):
    shape = jax.ShapeDtypeStruct((3, *own.shape[1:]), own.dtype)
    return pl.pallas_call(
        edges_kernel,
        in_specs=[ANY] * 4,
        out_specs=[ANY] * 2,
        out_shape=[shape, shape],
        scratch_shapes=[pltpu.SemaphoreType.DMA((6,))],
        name="edges",
    )(own, low_az, high_az, after)


def part_kernel(half, chosen, step_index, use, *refs):
    refs = list(refs)
    take = lambda wanted=True: refs.pop(0) if wanted else None
    table, blocks, own, low_az, high_az = (take() for _ in range(5))
    low_st, high_st = take(use["stream"]), take(use["stream"])
    other = take(use["basis"])
    take(use["before"])
    take(use["basis_before"])
    following, basis = take(), take(use["basis"])
    window, blocks_buf, result_buf, sems = (take() for _ in range(4))
    basis_buf, other_buf = take(use["basis"]), take(use["basis"])

    faces, width, depth = blocks.shape[1:]
    columns = own.shape[0]
    span = columns + 2
    rows, lanes = window.shape[1:]
    count = iter(range(sems.shape[0]))
    copy_of = lambda source, target: pltpu.make_async_copy(source, target, sems.at[next(count)])

    view = window.reshape(3, span, faces, rows, lanes)
    entering = []
    for azim, source in enumerate((low_az, own, high_az)):
        entering.append(copy_of(source, view.at[azim, pl.ds(1, columns)]))
        if use["stream"]:
            entering.append(copy_of(low_st.at[azim], view.at[azim, 0]))
            entering.append(copy_of(high_st.at[azim], view.at[azim, span - 1]))
    for copy in entering:
        copy.start()
    loading = [copy_of(blocks.at[column], blocks_buf.at[n]) for n, column in enumerate(chosen)]
    for copy in loading:
        copy.start()
    if use["basis"]:
        others = [copy_of(other.at[column], other_buf.at[n]) for n, column in enumerate(chosen)]
        for copy in others:
            copy.start()
        for copy in others:
            copy.wait()
    for copy in entering:
        copy.wait()

    neighbours = table.shape[1]
    low = low_lanes((rows, lanes))
    leaving = []
    for n, column in enumerate(chosen):
        loading[n].wait()
        for face in range(faces):
            gathered = jnp.concatenate(
                [window[table[face, k] + column * faces] for k in range(neighbours)], axis=0
            )
            block = blocks_buf[n, face]
            stacked = jnp.concatenate([block[:, : depth // 2], block[:, depth // 2 :]], axis=0)
            product = jnp.dot(stacked, gathered, preferred_element_type=jnp.float32)
            top, bottom = product[:width], product[width:]
            if half == 0:
                here = jnp.where(low, top[:rows], bottom[rows:])
                there = jnp.where(low, top[rows:], bottom[:rows])
            else:
                here = jnp.where(low, bottom[rows:], top[:rows])
                there = jnp.where(low, bottom[:rows], top[rows:])
            result = (here + swap_lanes(there)).astype(jnp.bfloat16)
            result_buf[n, face] = result
            if use["basis"]:
                upper, lower = unpacked(other_buf[n, face], result)
                basis_buf[n, face, :rows] = upper
                basis_buf[n, face, rows:] = lower
        leaving.append(copy_of(result_buf.at[n], following.at[column]))
        leaving[-1].start()
        if use["basis"]:
            leaving.append(copy_of(basis_buf.at[n], basis.at[step_index, column]))
            leaving[-1].start()
    for copy in leaving:
        copy.wait()


def part(half, index, chosen, table, blocks, pieces, stream=None, before=None, other=None, basis=None):
    columns, faces, width, depth = blocks.shape
    rows, lanes = pieces[0].shape[2:]
    use = {
        "stream": stream is not None,
        "basis": other is not None,
        "before": before is not None,
        "basis_before": basis is not None,
    }
    args = [table, blocks, *pieces]
    if stream is not None:
        args += stream
    if other is not None:
        args.append(other)
    aliases = {}
    if before is not None:
        aliases[len(args)] = 0
        args.append(before)
    if basis is not None:
        aliases[len(args)] = 1
        args.append(basis)
    out_shape = [jax.ShapeDtypeStruct((columns, faces, rows, lanes), jnp.bfloat16)]
    if other is not None:
        out_shape.append(jax.ShapeDtypeStruct((STEPS, columns, faces, width, lanes), jnp.bfloat16))
    size = len(chosen)
    scratch = [
        pltpu.VMEM((3 * (columns + 2) * faces, rows, lanes), jnp.bfloat16),
        pltpu.VMEM((size, faces, width, depth), jnp.bfloat16),
        pltpu.VMEM((size, faces, rows, lanes), jnp.bfloat16),
        pltpu.SemaphoreType.DMA((9 + 4 * size,)),
    ]
    if other is not None:
        scratch.append(pltpu.VMEM((size, faces, width, lanes), jnp.bfloat16))
        scratch.append(pltpu.VMEM((size, faces, rows, lanes), jnp.bfloat16))
    flops = 2 * size * faces * width * depth * lanes
    name = "edge" if stream is not None else "inner"
    return pl.pallas_call(
        functools.partial(part_kernel, half, chosen, index, use),
        in_specs=[pl.BlockSpec(memory_space=pltpu.SMEM)] + [ANY] * (len(args) - 1),
        out_specs=[ANY] * len(out_shape),
        out_shape=out_shape,
        input_output_aliases=aliases,
        scratch_shapes=scratch,
        cost_estimate=pl.CostEstimate(
            flops=flops, bytes_accessed=2 * size * faces * width * depth, transcendentals=0
        ),
        compiler_params=pltpu.CompilerParams(vmem_limit_bytes=VMEM_LIMIT),
        name=f"{name}_half{half}",
    )(*args)


def shift(value, axis, up):
    count = lax.axis_size(axis)
    pairs = [(i, (i + 1) % count) for i in range(count)]
    if not up:
        pairs = [(target, source) for source, target in pairs]
    return lax.ppermute(value, axis, pairs)


def halves_of_rows(blocks):
    columns, faces, width, depth = blocks.shape
    row = lax.broadcasted_iota(jnp.int32, (depth, depth), 0)
    column = lax.broadcasted_iota(jnp.int32, (depth, depth), 1)
    part_rows = width // 2
    place = (row // width) * part_rows + row % part_rows + ((row // part_rows) % 2) * (depth // 2)
    mover = (place == column).astype(jnp.bfloat16)
    moved = jnp.dot(blocks.reshape(-1, depth), mover, preferred_element_type=jnp.float32)
    return moved.astype(jnp.bfloat16).reshape(blocks.shape)


def local(start_vector, trace_blocks, neighbour):
    columns, around, faces, width, lanes = start_vector.shape
    start = start_vector.reshape(columns, faces, width, lanes)
    blocks = halves_of_rows(trace_blocks.reshape(columns, faces, width, -1))
    codes = neighbour.reshape(faces, -1)
    table = (((codes // faces) % 3) * (columns + 2) + codes // (3 * faces)) * faces + codes % faces
    inner = tuple(range(1, columns - 1))
    outer = (0, columns - 1)
    current = list(pack(start))
    basis = None
    latest = current[0]
    for index in range(STEPS):
        around_z = [
            (shift(current[h], "azim", True), shift(current[h], "azim", False))
            for h in range(HALVES)
        ]
        for h in range(HALVES):
            low_az, high_az = around_z[h]
            pieces = (current[h], low_az, high_az)
            to_low, to_high = edges(*pieces, latest)
            stream = [shift(to_high, "stream", True), shift(to_low, "stream", False)]
            last = index == STEPS - 1 and h == HALVES - 1
            other = current[0] if last else None
            outs = part(h, index, inner, table, blocks, pieces, other=other, basis=basis if last else None)
            outs = part(
                h, index, outer, table, blocks, pieces, stream=stream, before=outs[0],
                other=other, basis=outs[1] if last else None,
            )
            current[h] = latest = outs[0]
            if last:
                basis = outs[1]
        if index < STEPS - 1:
            basis = unpack(index, *current, basis)
    return basis.reshape(STEPS, columns, around, faces, width, lanes)


def solution(mesh):
    return jax.shard_map(
        local,
        mesh=mesh,
        in_specs=(
            P("stream", "azim", None, None, None),
            P("stream", "azim", None, None, None),
            P("azim", None, None),
        ),
        out_specs=P(None, "stream", "azim", None, None, None),
        check_vma=False,
    )
```

```python
import functools

import jax
import jax.numpy as jnp
from jax import lax
from jax.experimental import pallas as pl
from jax.experimental.pallas import tpu as pltpu
from jax.sharding import PartitionSpec as P

STEPS = 4
HALVES = 2
VMEM = pl.BlockSpec(memory_space=pltpu.VMEM)
ANY = pl.BlockSpec(memory_space=pl.ANY)


def low_lanes(shape):
    return lax.broadcasted_iota(jnp.int32, shape, len(shape) - 1) < shape[-1] // 2


def swap_lanes(value):
    return pltpu.roll(value, value.shape[-1] // 2, len(value.shape) - 1)


def pack_kernel(start_ref, first_ref, second_ref):
    columns, faces, width, lanes = start_ref.shape
    for column in range(columns):
        for face in range(faces):
            value = start_ref[column, face].astype(jnp.float32)
            top = value[: width // 2]
            bottom = swap_lanes(value[width // 2 :])
            low = low_lanes(top.shape)
            first_ref[column, face] = jnp.where(low, top, bottom).astype(jnp.bfloat16)
            second_ref[column, face] = jnp.where(low, bottom, top).astype(jnp.bfloat16)


def pack(start):
    columns, faces, width, lanes = start.shape
    half = jax.ShapeDtypeStruct((columns, faces, width // 2, lanes), jnp.bfloat16)
    return pl.pallas_call(
        pack_kernel,
        in_specs=[VMEM],
        out_specs=[VMEM] * 2,
        out_shape=[half, half],
        name="pack",
    )(start)


def unpack_kernel(index, chosen, skipped, first_ref, second_ref, *refs):
    basis_ref, done_ref, buffer, sems = refs[-4:]
    done_ref[...] = jnp.zeros_like(done_ref)
    faces, rows = first_ref.shape[1:3]
    copies = []
    for n, column in enumerate(chosen):
        for face in range(faces):
            first = first_ref[column, face].astype(jnp.float32)
            second = second_ref[column - skipped, face].astype(jnp.float32)
            low = low_lanes(first.shape)
            buffer[n, face, :rows] = jnp.where(low, first, second).astype(jnp.bfloat16)
            bottom = swap_lanes(jnp.where(low, second, first))
            buffer[n, face, rows:] = bottom.astype(jnp.bfloat16)
        copies.append(
            pltpu.make_async_copy(buffer.at[n], basis_ref.at[index, column], sems.at[n])
        )
        copies[-1].start()
    for copy in copies:
        copy.wait()


def unpack(index, chosen, first, second, basis, after):
    columns, faces, rows, lanes = first.shape
    size = len(chosen)
    skipped = 0 if second.shape[0] == columns else chosen[0]
    extra = [value for value in (basis, after) if value is not None]
    return pl.pallas_call(
        functools.partial(unpack_kernel, index, chosen, skipped),
        in_specs=[VMEM] * 2 + [ANY] * len(extra),
        out_specs=[ANY, VMEM],
        out_shape=[
            jax.ShapeDtypeStruct((STEPS, columns, faces, 2 * rows, lanes), jnp.bfloat16),
            jax.ShapeDtypeStruct((8, lanes), jnp.float32),
        ],
        scratch_shapes=[
            pltpu.VMEM((size, faces, 2 * rows, lanes), jnp.bfloat16),
            pltpu.SemaphoreType.DMA((size,)),
        ],
        input_output_aliases={} if basis is None else {2: 0},
        name="unpack",
    )(first, second, *extra)


def edges_kernel(own, low_az, high_az, after, to_low, to_high):
    columns = own.shape[0]
    for azim, source in enumerate((low_az, own, high_az)):
        to_low[azim] = source[0]
        to_high[azim] = source[columns - 1]


def edges(own, low_az, high_az, after):
    shape = jax.ShapeDtypeStruct((3, *own.shape[1:]), own.dtype)
    return pl.pallas_call(
        edges_kernel,
        in_specs=[VMEM] * 3 + [ANY],
        out_specs=[VMEM] * 2,
        out_shape=[shape, shape],
        name="edges",
    )(own, low_az, high_az, after)


def part_kernel(half, chosen, slots, *refs):
    window = refs[-1]
    following = refs[-2]
    table, blocks, own, low_az, high_az = refs[:5]
    faces, width, depth = blocks.shape[1:]
    columns = own.shape[0]
    span = columns + 2
    rows, lanes = window.shape[1:]
    view = window.reshape(3, span, faces, rows, lanes)
    for azim, source in enumerate((low_az, own, high_az)):
        view[azim, 1 : columns + 1] = source[...]
    if len(refs) > 7:
        low_st, high_st, before, after = refs[5:9]
        view[:, 0] = low_st[...]
        view[:, span - 1] = high_st[...]
        following[1 : columns - 1] = before[...]

    neighbours = table.shape[1]
    low = low_lanes((rows, lanes))
    for slot, column in zip(slots, chosen):
        for face in range(faces):
            gathered = jnp.concatenate(
                [window[table[face, k] + column * faces] for k in range(neighbours)], axis=0
            )
            block = blocks[column, face]
            stacked = jnp.concatenate([block[:, : depth // 2], block[:, depth // 2 :]], axis=0)
            product = jnp.dot(stacked, gathered, preferred_element_type=jnp.float32)
            top, bottom = product[:width], product[width:]
            if half == 0:
                here = jnp.where(low, top[:rows], bottom[rows:])
                there = jnp.where(low, top[rows:], bottom[:rows])
            else:
                here = jnp.where(low, bottom[rows:], top[:rows])
                there = jnp.where(low, bottom[:rows], top[rows:])
            following[slot, face] = (here + swap_lanes(there)).astype(jnp.bfloat16)


def part(half, chosen, table, blocks, pieces, stream=None, before=None, after=None):
    columns, faces, width, depth = blocks.shape
    rows, lanes = pieces[0].shape[2:]
    args = [table, blocks, *pieces]
    in_specs = [pl.BlockSpec(memory_space=pltpu.SMEM)] + [VMEM] * 4
    size = len(chosen)
    if stream is None:
        slots, out_columns = range(size), size
    else:
        slots, out_columns = chosen, columns
        args += [*stream, before, after]
        in_specs += [VMEM] * 3 + [ANY]
    name = "inner" if stream is None else "edge"
    return pl.pallas_call(
        functools.partial(part_kernel, half, chosen, slots),
        in_specs=in_specs,
        out_specs=VMEM,
        out_shape=jax.ShapeDtypeStruct((out_columns, faces, rows, lanes), jnp.bfloat16),
        scratch_shapes=[pltpu.VMEM((3 * (columns + 2) * faces, rows, lanes), jnp.bfloat16)],
        cost_estimate=pl.CostEstimate(
            flops=2 * size * faces * width * depth * lanes,
            bytes_accessed=2 * size * faces * width * depth,
            transcendentals=0,
        ),
        name=f"{name}_half{half}",
    )(*args)


def shift(value, axis, up):
    count = lax.axis_size(axis)
    pairs = [(i, (i + 1) % count) for i in range(count)]
    if not up:
        pairs = [(target, source) for source, target in pairs]
    return lax.ppermute(value, axis, pairs)


def halves_of_rows(blocks):
    columns, faces, width, depth = blocks.shape
    row = lax.broadcasted_iota(jnp.int32, (depth, depth), 0)
    column = lax.broadcasted_iota(jnp.int32, (depth, depth), 1)
    part_rows = width // 2
    place = (row // width) * part_rows + row % part_rows + ((row // part_rows) % 2) * (depth // 2)
    mover = (place == column).astype(jnp.bfloat16)
    moved = jnp.dot(blocks.reshape(-1, depth), mover, preferred_element_type=jnp.float32)
    return moved.astype(jnp.bfloat16).reshape(blocks.shape)


def local(start_vector, trace_blocks, neighbour):
    columns, around, faces, width, lanes = start_vector.shape
    start = start_vector.reshape(columns, faces, width, lanes)
    blocks = halves_of_rows(trace_blocks.reshape(columns, faces, width, -1))
    codes = neighbour.reshape(faces, -1)
    table = (((codes // faces) % 3) * (columns + 2) + codes // (3 * faces)) * faces + codes % faces
    inner = tuple(range(1, columns - 1))
    outer = (0, columns - 1)
    every = tuple(range(columns))
    current = list(pack(start))
    basis = None
    latest = current[0]
    for index in range(STEPS):
        around_z = [
            (shift(current[h], "azim", True), shift(current[h], "azim", False))
            for h in range(HALVES)
        ]
        previous = tuple(current)
        for h in range(HALVES):
            last = index == STEPS - 1 and h == HALVES - 1
            pieces = (current[h], *around_z[h])
            to_low, to_high = edges(*pieces, latest)
            stream = [shift(to_high, "stream", True), shift(to_low, "stream", False)]
            middle = part(h, inner, table, blocks, pieces)
            after = middle
            if h == 0 and index > 0:
                basis, after = unpack(index - 1, every, *previous, basis, middle)
            if last:
                basis, after = unpack(index, inner, current[0], middle, basis, None)
            current[h] = latest = part(h, outer, table, blocks, pieces, stream, middle, after)
    basis, _ = unpack(STEPS - 1, outer, *current, basis, None)
    return basis.reshape(STEPS, columns, around, faces, width, lanes)


def solution(mesh):
    return jax.shard_map(
        local,
        mesh=mesh,
        in_specs=(
            P("stream", "azim", None, None, None),
            P("stream", "azim", None, None, None),
            P("azim", None, None),
        ),
        out_specs=P(None, "stream", "azim", None, None, None),
        check_vma=False,
    )
```

```python
import functools

import jax
import jax.numpy as jnp
from jax import lax
from jax.experimental import pallas as pl
from jax.experimental.pallas import tpu as pltpu
from jax.sharding import PartitionSpec as P

STEPS = 4
HALVES = 2
VMEM = pl.BlockSpec(memory_space=pltpu.VMEM)
ANY = pl.BlockSpec(memory_space=pl.ANY)


def low_lanes(shape):
    return lax.broadcasted_iota(jnp.int32, shape, len(shape) - 1) < shape[-1] // 2


def swap_lanes(value):
    return pltpu.roll(value, value.shape[-1] // 2, len(value.shape) - 1)


def pack_kernel(start_ref, first_ref, second_ref):
    columns, faces, width, lanes = start_ref.shape
    for column in range(columns):
        for face in range(faces):
            value = start_ref[column, face].astype(jnp.float32)
            top = value[: width // 2]
            bottom = swap_lanes(value[width // 2 :])
            low = low_lanes(top.shape)
            first_ref[column, face] = jnp.where(low, top, bottom).astype(jnp.bfloat16)
            second_ref[column, face] = jnp.where(low, bottom, top).astype(jnp.bfloat16)


def pack(start):
    columns, faces, width, lanes = start.shape
    half = jax.ShapeDtypeStruct((columns, faces, width // 2, lanes), jnp.bfloat16)
    return pl.pallas_call(
        pack_kernel,
        in_specs=[VMEM],
        out_specs=[VMEM] * 2,
        out_shape=[half, half],
        name="pack",
    )(start)


def unpack_kernel(index, chosen, skipped, first_ref, second_ref, *refs):
    basis_ref, done_ref, buffer, sems = refs[-4:]
    done_ref[...] = jnp.zeros_like(done_ref)
    faces, rows = first_ref.shape[1:3]
    copies = []
    for n, column in enumerate(chosen):
        for face in range(faces):
            first = first_ref[column, face].astype(jnp.float32)
            second = second_ref[column - skipped, face].astype(jnp.float32)
            low = low_lanes(first.shape)
            buffer[n, face, :rows] = jnp.where(low, first, second).astype(jnp.bfloat16)
            bottom = swap_lanes(jnp.where(low, second, first))
            buffer[n, face, rows:] = bottom.astype(jnp.bfloat16)
        copies.append(
            pltpu.make_async_copy(buffer.at[n], basis_ref.at[index, column], sems.at[n])
        )
        copies[-1].start()
    for copy in copies:
        copy.wait()


def unpack(index, chosen, first, second, basis, after):
    columns, faces, rows, lanes = first.shape
    size = len(chosen)
    skipped = 0 if second.shape[0] == columns else chosen[0]
    extra = [value for value in (basis, after) if value is not None]
    return pl.pallas_call(
        functools.partial(unpack_kernel, index, chosen, skipped),
        in_specs=[VMEM] * 2 + [ANY] * len(extra),
        out_specs=[ANY, VMEM],
        out_shape=[
            jax.ShapeDtypeStruct((STEPS, columns, faces, 2 * rows, lanes), jnp.bfloat16),
            jax.ShapeDtypeStruct((8, lanes), jnp.float32),
        ],
        scratch_shapes=[
            pltpu.VMEM((size, faces, 2 * rows, lanes), jnp.bfloat16),
            pltpu.SemaphoreType.DMA((size,)),
        ],
        input_output_aliases={} if basis is None else {2: 0},
        name="unpack",
    )(first, second, *extra)


def edges(own, low_az, high_az, after):
    *trio, _ = lax.optimization_barrier((low_az, own, high_az, after))
    columns = own.shape[0]
    return jnp.stack([part[0] for part in trio]), jnp.stack([part[columns - 1] for part in trio])


def step_kernel(half, table, blocks, own, low_az, high_az, low_st, high_st, after, following, window):
    faces, width, depth = blocks.shape[1:]
    columns = own.shape[0]
    span = columns + 2
    rows, lanes = window.shape[1:]
    view = window.reshape(3, span, faces, rows, lanes)
    for azim, source in enumerate((low_az, own, high_az)):
        view[azim, 1 : columns + 1] = source[...]
    view[:, 0] = low_st[...]
    view[:, span - 1] = high_st[...]
    neighbours = table.shape[1]
    low = low_lanes((rows, lanes))

    def one(column, face):
        gathered = jnp.concatenate(
            [window[table[face, k] + column * faces] for k in range(neighbours)], axis=0
        )
        block = blocks[column, face]
        stacked = jnp.concatenate([block[:, : depth // 2], block[:, depth // 2 :]], axis=0)
        product = jnp.dot(stacked, gathered, preferred_element_type=jnp.float32)
        top, bottom = product[:width], product[width:]
        if half == 0:
            here = jnp.where(low, top[:rows], bottom[rows:])
            there = jnp.where(low, top[rows:], bottom[:rows])
        else:
            here = jnp.where(low, bottom[rows:], top[:rows])
            there = jnp.where(low, bottom[:rows], top[rows:])
        following[column, face] = (here + swap_lanes(there)).astype(jnp.bfloat16)

    def turn(column, carry):
        for face in range(faces):
            one(column, face)
        return carry

    lax.fori_loop(0, columns, turn, 0)


def step(half, table, blocks, pieces, stream, after):
    columns, faces, width, depth = blocks.shape
    rows, lanes = pieces[0].shape[2:]
    return pl.pallas_call(
        functools.partial(step_kernel, half),
        in_specs=[pl.BlockSpec(memory_space=pltpu.SMEM)] + [VMEM] * 6 + [ANY],
        out_specs=VMEM,
        out_shape=jax.ShapeDtypeStruct((columns, faces, rows, lanes), jnp.bfloat16),
        scratch_shapes=[pltpu.VMEM((3 * (columns + 2) * faces, rows, lanes), jnp.bfloat16)],
        cost_estimate=pl.CostEstimate(
            flops=2 * columns * faces * width * depth * lanes,
            bytes_accessed=2 * columns * faces * width * depth,
            transcendentals=0,
        ),
        name=f"step_half{half}",
    )(table, blocks, *pieces, *stream, after)


def shift(value, axis, up):
    count = lax.axis_size(axis)
    pairs = [(i, (i + 1) % count) for i in range(count)]
    if not up:
        pairs = [(target, source) for source, target in pairs]
    return lax.ppermute(value, axis, pairs)


def halves_of_rows(blocks):
    columns, faces, width, depth = blocks.shape
    row = lax.broadcasted_iota(jnp.int32, (depth, depth), 0)
    column = lax.broadcasted_iota(jnp.int32, (depth, depth), 1)
    part_rows = width // 2
    place = (row // width) * part_rows + row % part_rows + ((row // part_rows) % 2) * (depth // 2)
    mover = (place == column).astype(jnp.bfloat16)
    moved = jnp.dot(blocks.reshape(-1, depth), mover, preferred_element_type=jnp.float32)
    return moved.astype(jnp.bfloat16).reshape(blocks.shape)


def local(start_vector, trace_blocks, neighbour):
    columns, around, faces, width, lanes = start_vector.shape
    start = start_vector.reshape(columns, faces, width, lanes)
    blocks = halves_of_rows(trace_blocks.reshape(columns, faces, width, -1))
    codes = neighbour.reshape(faces, -1)
    table = (((codes // faces) % 3) * (columns + 2) + codes // (3 * faces)) * faces + codes % faces
    every = tuple(range(columns))
    current = list(pack(start))
    basis = None
    latest = current[0]
    for index in range(STEPS):
        around_z = [
            (shift(current[h], "azim", True), shift(current[h], "azim", False))
            for h in range(HALVES)
        ]
        previous = tuple(current)
        for h in range(HALVES):
            pieces = (current[h], *around_z[h])
            to_low, to_high = edges(*pieces, latest)
            stream = [shift(to_high, "stream", True), shift(to_low, "stream", False)]
            if h == 1 and index > 0:
                basis, latest = unpack(index - 1, every, *previous, basis, latest)
            current[h] = latest = step(h, table, blocks, pieces, stream, latest)
    basis, _ = unpack(STEPS - 1, every, *current, basis, None)
    return basis.reshape(STEPS, columns, around, faces, width, lanes)


def solution(mesh):
    return jax.shard_map(
        local,
        mesh=mesh,
        in_specs=(
            P("stream", "azim", None, None, None),
            P("stream", "azim", None, None, None),
            P("azim", None, None),
        ),
        out_specs=P(None, "stream", "azim", None, None, None),
        check_vma=False,
    )
```

```python
import functools

import jax
import jax.numpy as jnp
from jax import lax
from jax.experimental import pallas as pl
from jax.experimental.pallas import tpu as pltpu
from jax.sharding import PartitionSpec as P

STEPS = 4
HALVES = 2
VMEM_LIMIT = 4 * 1024 * 1024
VMEM = pl.BlockSpec(memory_space=pltpu.VMEM)
ANY = pl.BlockSpec(memory_space=pl.ANY)


def low_lanes(shape):
    return lax.broadcasted_iota(jnp.int32, shape, len(shape) - 1) < shape[-1] // 2


def swap_lanes(value):
    return pltpu.roll(value, value.shape[-1] // 2, len(value.shape) - 1)


def pack_kernel(start_ref, first_ref, second_ref):
    columns, faces, width, lanes = start_ref.shape
    for column in range(columns):
        for face in range(faces):
            value = start_ref[column, face].astype(jnp.float32)
            top = value[: width // 2]
            bottom = swap_lanes(value[width // 2 :])
            low = low_lanes(top.shape)
            first_ref[column, face] = jnp.where(low, top, bottom).astype(jnp.bfloat16)
            second_ref[column, face] = jnp.where(low, bottom, top).astype(jnp.bfloat16)


def pack(start):
    columns, faces, width, lanes = start.shape
    half = jax.ShapeDtypeStruct((columns, faces, width // 2, lanes), jnp.bfloat16)
    return pl.pallas_call(
        pack_kernel,
        in_specs=[VMEM],
        out_specs=[VMEM] * 2,
        out_shape=[half, half],
        compiler_params=pltpu.CompilerParams(vmem_limit_bytes=VMEM_LIMIT),
        name="pack",
    )(start)


def unpack_kernel(index, chosen, skipped, first_ref, second_ref, *refs):
    basis_ref, done_ref, buffer, sems = refs[-4:]
    done_ref[...] = jnp.zeros_like(done_ref)
    faces, rows = first_ref.shape[1:3]
    copies = []
    for n, column in enumerate(chosen):
        for face in range(faces):
            first = first_ref[column, face].astype(jnp.float32)
            second = second_ref[column - skipped, face].astype(jnp.float32)
            low = low_lanes(first.shape)
            buffer[n, face, :rows] = jnp.where(low, first, second).astype(jnp.bfloat16)
            bottom = swap_lanes(jnp.where(low, second, first))
            buffer[n, face, rows:] = bottom.astype(jnp.bfloat16)
        copies.append(
            pltpu.make_async_copy(buffer.at[n], basis_ref.at[index, column], sems.at[n])
        )
        copies[-1].start()
    for copy in copies:
        copy.wait()


def unpack(index, chosen, first, second, basis, after):
    columns, faces, rows, lanes = first.shape
    size = len(chosen)
    skipped = 0 if second.shape[0] == columns else chosen[0]
    extra = [value for value in (basis, after) if value is not None]
    return pl.pallas_call(
        functools.partial(unpack_kernel, index, chosen, skipped),
        in_specs=[VMEM] * 2 + [ANY] * len(extra),
        out_specs=[ANY, VMEM],
        out_shape=[
            jax.ShapeDtypeStruct((STEPS, columns, faces, 2 * rows, lanes), jnp.bfloat16),
            jax.ShapeDtypeStruct((8, lanes), jnp.float32),
        ],
        scratch_shapes=[
            pltpu.VMEM((size, faces, 2 * rows, lanes), jnp.bfloat16),
            pltpu.SemaphoreType.DMA((size,)),
        ],
        input_output_aliases={} if basis is None else {2: 0},
        compiler_params=pltpu.CompilerParams(vmem_limit_bytes=VMEM_LIMIT),
        name="unpack",
    )(first, second, *extra)


def edges(own, low_az, high_az, after):
    *trio, _ = lax.optimization_barrier((low_az, own, high_az, after))
    columns = own.shape[0]
    return jnp.stack([part[0] for part in trio]), jnp.stack([part[columns - 1] for part in trio])


def step_kernel(half, table, blocks, own, low_az, high_az, low_st, high_st, after, following, window):
    faces, width, depth = blocks.shape[1:]
    columns = own.shape[0]
    span = columns + 2
    rows, lanes = window.shape[1:]
    view = window.reshape(3, span, faces, rows, lanes)
    for azim, source in enumerate((low_az, own, high_az)):
        view[azim, 1 : columns + 1] = source[...]
    view[:, 0] = low_st[...]
    view[:, span - 1] = high_st[...]
    neighbours = table.shape[1]
    low = low_lanes((rows, lanes))

    def one(column, face):
        gathered = jnp.concatenate(
            [window[table[face, k] + column * faces] for k in range(neighbours)], axis=0
        )
        block = blocks[column, face]
        stacked = jnp.concatenate([block[:, : depth // 2], block[:, depth // 2 :]], axis=0)
        product = jnp.dot(stacked, gathered, preferred_element_type=jnp.float32)
        top, bottom = product[:width], product[width:]
        if half == 0:
            here = jnp.where(low, top[:rows], bottom[rows:])
            there = jnp.where(low, top[rows:], bottom[:rows])
        else:
            here = jnp.where(low, bottom[rows:], top[:rows])
            there = jnp.where(low, bottom[:rows], top[rows:])
        following[column, face] = (here + swap_lanes(there)).astype(jnp.bfloat16)

    def turn(column, carry):
        for face in range(faces):
            one(column, face)
        return carry

    lax.fori_loop(0, columns, turn, 0)


def step(half, table, blocks, pieces, stream, after):
    columns, faces, width, depth = blocks.shape
    rows, lanes = pieces[0].shape[2:]
    return pl.pallas_call(
        functools.partial(step_kernel, half),
        in_specs=[pl.BlockSpec(memory_space=pltpu.SMEM)] + [VMEM] * 6 + [ANY],
        out_specs=VMEM,
        out_shape=jax.ShapeDtypeStruct((columns, faces, rows, lanes), jnp.bfloat16),
        scratch_shapes=[pltpu.VMEM((3 * (columns + 2) * faces, rows, lanes), jnp.bfloat16)],
        cost_estimate=pl.CostEstimate(
            flops=2 * columns * faces * width * depth * lanes,
            bytes_accessed=2 * columns * faces * width * depth,
            transcendentals=0,
        ),
        compiler_params=pltpu.CompilerParams(vmem_limit_bytes=VMEM_LIMIT),
        name=f"step_half{half}",
    )(table, blocks, *pieces, *stream, after)


def shift(value, axis, up):
    count = lax.axis_size(axis)
    pairs = [(i, (i + 1) % count) for i in range(count)]
    if not up:
        pairs = [(target, source) for source, target in pairs]
    return lax.ppermute(value, axis, pairs)


def halves_of_rows(blocks):
    columns, faces, width, depth = blocks.shape
    row = lax.broadcasted_iota(jnp.int32, (depth, depth), 0)
    column = lax.broadcasted_iota(jnp.int32, (depth, depth), 1)
    part_rows = width // 2
    place = (row // width) * part_rows + row % part_rows + ((row // part_rows) % 2) * (depth // 2)
    mover = (place == column).astype(jnp.bfloat16)
    moved = jnp.dot(blocks.reshape(-1, depth), mover, preferred_element_type=jnp.float32)
    return moved.astype(jnp.bfloat16).reshape(blocks.shape)


def local(start_vector, trace_blocks, neighbour):
    columns, around, faces, width, lanes = start_vector.shape
    start = start_vector.reshape(columns, faces, width, lanes)
    blocks = halves_of_rows(trace_blocks.reshape(columns, faces, width, -1))
    codes = neighbour.reshape(faces, -1)
    table = (((codes // faces) % 3) * (columns + 2) + codes // (3 * faces)) * faces + codes % faces
    every = tuple(range(columns))
    current = list(pack(start))
    basis = None
    latest = current[0]
    for index in range(STEPS):
        around_z = [
            (shift(current[h], "azim", True), shift(current[h], "azim", False))
            for h in range(HALVES)
        ]
        previous = tuple(current)
        for h in range(HALVES):
            pieces = (current[h], *around_z[h])
            to_low, to_high = edges(*pieces, latest)
            stream = [shift(to_high, "stream", True), shift(to_low, "stream", False)]
            if h == 1 and index > 0:
                basis, latest = unpack(index - 1, every, *previous, basis, latest)
            current[h] = latest = step(h, table, blocks, pieces, stream, latest)
    basis, _ = unpack(STEPS - 1, every, *current, basis, None)
    return basis.reshape(STEPS, columns, around, faces, width, lanes)


def solution(mesh):
    return jax.shard_map(
        local,
        mesh=mesh,
        in_specs=(
            P("stream", "azim", None, None, None),
            P("stream", "azim", None, None, None),
            P("azim", None, None),
        ),
        out_specs=P(None, "stream", "azim", None, None, None),
        check_vma=False,
    )
```

```python
import functools

import jax
import jax.numpy as jnp
from jax import lax
from jax.experimental import pallas as pl
from jax.experimental.pallas import tpu as pltpu
from jax.sharding import PartitionSpec as P

STEPS = 4
HALVES = 2
VMEM_LIMIT = 4 * 1024 * 1024
VMEM = pl.BlockSpec(memory_space=pltpu.VMEM)
ANY = pl.BlockSpec(memory_space=pl.ANY)


def low_lanes(shape):
    return lax.broadcasted_iota(jnp.int32, shape, len(shape) - 1) < shape[-1] // 2


def swap_lanes(value):
    return pltpu.roll(value, value.shape[-1] // 2, len(value.shape) - 1)


def pack_kernel(start_ref, first_ref, second_ref):
    columns, faces, width, lanes = start_ref.shape
    for column in range(columns):
        for face in range(faces):
            value = start_ref[column, face].astype(jnp.float32)
            top = value[: width // 2]
            bottom = swap_lanes(value[width // 2 :])
            low = low_lanes(top.shape)
            first_ref[column, face] = jnp.where(low, top, bottom).astype(jnp.bfloat16)
            second_ref[column, face] = jnp.where(low, bottom, top).astype(jnp.bfloat16)


def pack(start):
    columns, faces, width, lanes = start.shape
    half = jax.ShapeDtypeStruct((columns, faces, width // 2, lanes), jnp.bfloat16)
    return pl.pallas_call(
        pack_kernel,
        in_specs=[VMEM],
        out_specs=[VMEM] * 2,
        out_shape=[half, half],
        compiler_params=pltpu.CompilerParams(vmem_limit_bytes=VMEM_LIMIT),
        name="pack",
    )(start)


def unpack_kernel(index, chosen, skipped, first_ref, second_ref, *refs):
    basis_ref, done_ref, buffer, sems = refs[-4:]
    done_ref[...] = jnp.zeros_like(done_ref)
    faces, rows = first_ref.shape[1:3]
    copies = []
    for n, column in enumerate(chosen):
        for face in range(faces):
            first = first_ref[column, face].astype(jnp.float32)
            second = second_ref[column - skipped, face].astype(jnp.float32)
            low = low_lanes(first.shape)
            buffer[n, face, :rows] = jnp.where(low, first, second).astype(jnp.bfloat16)
            bottom = swap_lanes(jnp.where(low, second, first))
            buffer[n, face, rows:] = bottom.astype(jnp.bfloat16)
        copies.append(
            pltpu.make_async_copy(buffer.at[n], basis_ref.at[index, column], sems.at[n])
        )
        copies[-1].start()
    for copy in copies:
        copy.wait()


def unpack(index, chosen, first, second, basis, after):
    columns, faces, rows, lanes = first.shape
    size = len(chosen)
    skipped = 0 if second.shape[0] == columns else chosen[0]
    extra = [value for value in (basis, after) if value is not None]
    return pl.pallas_call(
        functools.partial(unpack_kernel, index, chosen, skipped),
        in_specs=[VMEM] * 2 + [ANY] * len(extra),
        out_specs=[ANY, VMEM],
        out_shape=[
            jax.ShapeDtypeStruct((STEPS, columns, faces, 2 * rows, lanes), jnp.bfloat16),
            jax.ShapeDtypeStruct((8, lanes), jnp.float32),
        ],
        scratch_shapes=[
            pltpu.VMEM((size, faces, 2 * rows, lanes), jnp.bfloat16),
            pltpu.SemaphoreType.DMA((size,)),
        ],
        input_output_aliases={} if basis is None else {2: 0},
        compiler_params=pltpu.CompilerParams(vmem_limit_bytes=VMEM_LIMIT),
        name="unpack",
    )(first, second, *extra)


def edges(own, low_az, high_az, after):
    *trio, _ = lax.optimization_barrier((low_az, own, high_az, after))
    columns = own.shape[0]
    return jnp.stack([part[0] for part in trio]), jnp.stack([part[columns - 1] for part in trio])


def part_kernel(half, *refs):
    table, blocks, own, low_az, high_az = refs[:5]
    following, window = refs[-2:]
    edge = len(refs) > 9
    faces, width, depth = blocks.shape[1:]
    columns = own.shape[0]
    span = columns + 2
    rows, lanes = window.shape[1:]
    view = window.reshape(3, span, faces, rows, lanes)

    def enter(column, carry):
        for azim, source in enumerate((low_az, own, high_az)):
            for face in range(faces):
                view[azim, column + 1, face] = source[column, face]
        return carry

    lax.fori_loop(0, columns, enter, 0)
    if edge:
        low_st, high_st, before = refs[5:8]

        def enter_stream(face, carry):
            for azim in range(3):
                view[azim, 0, face] = low_st[azim, face]
                view[azim, span - 1, face] = high_st[azim, face]
            for column in range(columns - 2):
                following[column + 1, face] = before[column, face]
            return carry

        lax.fori_loop(0, faces, enter_stream, 0)
    neighbours = table.shape[1]
    low = low_lanes((rows, lanes))

    def turn(n, carry):
        column = n * (columns - 1) if edge else n + 1
        slot = column if edge else n
        for face in range(faces):
            gathered = jnp.concatenate(
                [window[table[face, k] + column * faces] for k in range(neighbours)], axis=0
            )
            block = blocks[column, face]
            stacked = jnp.concatenate([block[:, : depth // 2], block[:, depth // 2 :]], axis=0)
            product = jnp.dot(stacked, gathered, preferred_element_type=jnp.float32)
            top, bottom = product[:width], product[width:]
            if half == 0:
                here = jnp.where(low, top[:rows], bottom[rows:])
                there = jnp.where(low, top[rows:], bottom[:rows])
            else:
                here = jnp.where(low, bottom[rows:], top[:rows])
                there = jnp.where(low, bottom[:rows], top[rows:])
            following[slot, face] = (here + swap_lanes(there)).astype(jnp.bfloat16)
        return carry

    lax.fori_loop(0, 2 if edge else columns - 2, turn, 0)


def part(half, table, blocks, pieces, rest):
    columns, faces, width, depth = blocks.shape
    rows, lanes = pieces[0].shape[2:]
    edge = len(rest) > 2
    name = "edge" if edge else "inner"
    done, kept = (2, columns) if edge else (columns - 2, columns - 2)
    in_specs = [pl.BlockSpec(memory_space=pltpu.SMEM)] + [VMEM] * 4
    in_specs += [VMEM] * 3 + [ANY] if edge else [ANY] * 2
    return pl.pallas_call(
        functools.partial(part_kernel, half),
        in_specs=in_specs,
        out_specs=VMEM,
        out_shape=jax.ShapeDtypeStruct((kept, faces, rows, lanes), jnp.bfloat16),
        scratch_shapes=[pltpu.VMEM((3 * (columns + 2) * faces, rows, lanes), jnp.bfloat16)],
        cost_estimate=pl.CostEstimate(
            flops=2 * done * faces * width * depth * lanes,
            bytes_accessed=2 * done * faces * width * depth,
            transcendentals=0,
        ),
        compiler_params=pltpu.CompilerParams(vmem_limit_bytes=VMEM_LIMIT),
        name=f"{name}_half{half}",
    )(table, blocks, *pieces, *rest)


def shift(value, axis, up):
    count = lax.axis_size(axis)
    pairs = [(i, (i + 1) % count) for i in range(count)]
    if not up:
        pairs = [(target, source) for source, target in pairs]
    return lax.ppermute(value, axis, pairs)


def halves_kernel(blocks, moved):
    columns, faces, width, depth = blocks.shape
    part_rows = width // 2
    group = 4 * width
    row = lax.broadcasted_iota(jnp.int32, (group, group), 0)
    column = lax.broadcasted_iota(jnp.int32, (group, group), 1)
    place = (row // width) * part_rows + row % part_rows
    place = place + ((row // part_rows) % 2) * (group // 2)
    mover = jnp.where(place == column, 1.0, 0.0).astype(jnp.bfloat16)

    def turn(n, carry):
        for face in range(faces):
            for first in range(0, depth, group):
                result = jnp.dot(
                    blocks[n, face, :, first : first + group],
                    mover,
                    preferred_element_type=jnp.float32,
                ).astype(jnp.bfloat16)
                at = first // 2
                moved[n, face, :, at : at + group // 2] = result[:, : group // 2]
                at += depth // 2
                moved[n, face, :, at : at + group // 2] = result[:, group // 2 :]
        return carry

    lax.fori_loop(0, columns, turn, 0)


def halves_of_rows(blocks):
    return pl.pallas_call(
        halves_kernel,
        in_specs=[VMEM],
        out_specs=VMEM,
        out_shape=jax.ShapeDtypeStruct(blocks.shape, blocks.dtype),
        compiler_params=pltpu.CompilerParams(vmem_limit_bytes=VMEM_LIMIT),
        name="halves_of_rows",
    )(blocks)


def local(start_vector, trace_blocks, neighbour):
    columns, around, faces, width, lanes = start_vector.shape
    start = start_vector.reshape(columns, faces, width, lanes)
    blocks = halves_of_rows(trace_blocks.reshape(columns, faces, width, -1))
    codes = neighbour.reshape(faces, -1)
    table = (((codes // faces) % 3) * (columns + 2) + codes // (3 * faces)) * faces + codes % faces
    every = tuple(range(columns))
    current = list(pack(start))
    basis = None
    latest = current[0]
    lows = [shift(current[h], "azim", True) for h in range(HALVES)]
    highs = [shift(current[h], "azim", False) for h in range(HALVES)]
    for index in range(STEPS):
        previous = tuple(current)
        for h in range(HALVES):
            pieces = (current[h], lows[h], highs[h])
            to_low, to_high = edges(*pieces, latest)
            stream = (shift(to_high, "stream", True), shift(to_low, "stream", False))
            middle = part(h, table, blocks, pieces, (to_low, to_high))
            after = middle
            if h == 1 and index > 0:
                basis, after = unpack(index - 1, every, *previous, basis, middle)
            current[h] = latest = part(h, table, blocks, pieces, (*stream, middle, after))
            if index < STEPS - 1:
                lows[h] = shift(current[h], "azim", True)
                highs[h] = shift(current[h], "azim", False)
    basis, _ = unpack(STEPS - 1, every, *current, basis, None)
    return basis.reshape(STEPS, columns, around, faces, width, lanes)


def solution(mesh):
    return jax.shard_map(
        local,
        mesh=mesh,
        in_specs=(
            P("stream", "azim", None, None, None),
            P("stream", "azim", None, None, None),
            P("azim", None, None),
        ),
        out_specs=P(None, "stream", "azim", None, None, None),
        check_vma=False,
    )
```

```python
import functools

import jax
import jax.numpy as jnp
from jax import lax
from jax.experimental import pallas as pl
from jax.experimental.pallas import tpu as pltpu
from jax.sharding import PartitionSpec as P

STEPS = 4
HALVES = 2
WEIGHT = 100
VMEM_LIMIT = 4 * 1024 * 1024
VMEM = pl.BlockSpec(memory_space=pltpu.VMEM)
ANY = pl.BlockSpec(memory_space=pl.ANY)


def low_lanes(shape):
    return lax.broadcasted_iota(jnp.int32, shape, len(shape) - 1) < shape[-1] // 2


def swap_lanes(value):
    return pltpu.roll(value, value.shape[-1] // 2, len(value.shape) - 1)


def pack_kernel(start_ref, first_ref, second_ref):
    columns, faces, width, lanes = start_ref.shape
    for column in range(columns):
        for face in range(faces):
            value = start_ref[column, face].astype(jnp.float32)
            top = value[: width // 2]
            bottom = swap_lanes(value[width // 2 :])
            low = low_lanes(top.shape)
            first_ref[column, face] = jnp.where(low, top, bottom).astype(jnp.bfloat16)
            second_ref[column, face] = jnp.where(low, bottom, top).astype(jnp.bfloat16)


def pack(start):
    columns, faces, width, lanes = start.shape
    half = jax.ShapeDtypeStruct((columns, faces, width // 2, lanes), jnp.bfloat16)
    return pl.pallas_call(
        pack_kernel,
        in_specs=[VMEM],
        out_specs=[VMEM] * 2,
        out_shape=[half, half],
        compiler_params=pltpu.CompilerParams(vmem_limit_bytes=VMEM_LIMIT),
        name="pack",
    )(start)


def unpack_kernel(index, chosen, skipped, first_ref, second_ref, *refs):
    basis_ref, done_ref, buffer, sems = refs[-4:]
    done_ref[...] = jnp.zeros_like(done_ref)
    faces, rows = first_ref.shape[1:3]
    copies = []
    for n, column in enumerate(chosen):
        for face in range(faces):
            first = first_ref[column, face].astype(jnp.float32)
            second = second_ref[column - skipped, face].astype(jnp.float32)
            low = low_lanes(first.shape)
            buffer[n, face, :rows] = jnp.where(low, first, second).astype(jnp.bfloat16)
            bottom = swap_lanes(jnp.where(low, second, first))
            buffer[n, face, rows:] = bottom.astype(jnp.bfloat16)
        copies.append(
            pltpu.make_async_copy(buffer.at[n], basis_ref.at[index, column], sems.at[n])
        )
        copies[-1].start()
    for copy in copies:
        copy.wait()


def unpack(index, chosen, first, second, basis, after):
    columns, faces, rows, lanes = first.shape
    size = len(chosen)
    skipped = 0 if second.shape[0] == columns else chosen[0]
    extra = [value for value in (basis, after) if value is not None]
    return pl.pallas_call(
        functools.partial(unpack_kernel, index, chosen, skipped),
        in_specs=[VMEM] * 2 + [ANY] * len(extra),
        out_specs=[ANY, VMEM],
        out_shape=[
            jax.ShapeDtypeStruct((STEPS, columns, faces, 2 * rows, lanes), jnp.bfloat16),
            jax.ShapeDtypeStruct((8, lanes), jnp.float32),
        ],
        scratch_shapes=[
            pltpu.VMEM((size, faces, 2 * rows, lanes), jnp.bfloat16),
            pltpu.SemaphoreType.DMA((size,)),
        ],
        input_output_aliases={} if basis is None else {2: 0},
        compiler_params=pltpu.CompilerParams(vmem_limit_bytes=VMEM_LIMIT),
        name="unpack",
    )(first, second, *extra)


def edges(own, low_az, high_az, after):
    *trio, _ = lax.optimization_barrier((low_az, own, high_az, after))
    columns = own.shape[0]
    return jnp.stack([part[0] for part in trio]), jnp.stack([part[columns - 1] for part in trio])


def part_kernel(half, *refs):
    table, blocks, own, low_az, high_az = refs[:5]
    following, window = refs[-2:]
    edge = len(refs) > 9
    faces, width, depth = blocks.shape[1:]
    columns = own.shape[0]
    span = columns + 2
    rows, lanes = window.shape[1:]
    view = window.reshape(3, span, faces, rows, lanes)

    def enter(column, carry):
        for azim, source in enumerate((low_az, own, high_az)):
            for face in range(faces):
                view[azim, column + 1, face] = source[column, face]
        return carry

    lax.fori_loop(0, columns, enter, 0)
    if edge:
        low_st, high_st, before = refs[5:8]

        def enter_stream(face, carry):
            for azim in range(3):
                view[azim, 0, face] = low_st[azim, face]
                view[azim, span - 1, face] = high_st[azim, face]
            for column in range(columns - 2):
                following[column + 1, face] = before[column, face]
            return carry

        lax.fori_loop(0, faces, enter_stream, 0)
    neighbours = table.shape[1]
    low = low_lanes((rows, lanes))

    def turn(n, carry):
        column = n * (columns - 1) if edge else n + 1
        slot = column if edge else n
        for face in range(faces):
            gathered = jnp.concatenate(
                [window[table[face, k] + column * faces] for k in range(neighbours)], axis=0
            )
            block = blocks[column, face]
            stacked = jnp.concatenate([block[:, : depth // 2], block[:, depth // 2 :]], axis=0)
            product = jnp.dot(stacked, gathered, preferred_element_type=jnp.float32)
            top, bottom = product[:width], product[width:]
            if half == 0:
                here = jnp.where(low, top[:rows], bottom[rows:])
                there = jnp.where(low, top[rows:], bottom[:rows])
            else:
                here = jnp.where(low, bottom[rows:], top[:rows])
                there = jnp.where(low, bottom[:rows], top[rows:])
            following[slot, face] = (here + swap_lanes(there)).astype(jnp.bfloat16)
        return carry

    lax.fori_loop(0, 2 if edge else columns - 2, turn, 0)


def part(half, table, blocks, pieces, rest):
    columns, faces, width, depth = blocks.shape
    rows, lanes = pieces[0].shape[2:]
    edge = len(rest) > 2
    name = "edge" if edge else "inner"
    done, kept = (2, columns) if edge else (columns - 2, columns - 2)
    in_specs = [pl.BlockSpec(memory_space=pltpu.SMEM)] + [VMEM] * 4
    in_specs += [VMEM] * 3 + [ANY] if edge else [ANY] * 2
    return pl.pallas_call(
        functools.partial(part_kernel, half),
        in_specs=in_specs,
        out_specs=VMEM,
        out_shape=jax.ShapeDtypeStruct((kept, faces, rows, lanes), jnp.bfloat16),
        scratch_shapes=[pltpu.VMEM((3 * (columns + 2) * faces, rows, lanes), jnp.bfloat16)],
        cost_estimate=pl.CostEstimate(
            flops=WEIGHT * 2 * done * faces * width * depth * lanes,
            bytes_accessed=2 * done * faces * width * depth,
            transcendentals=0,
        ),
        compiler_params=pltpu.CompilerParams(vmem_limit_bytes=VMEM_LIMIT),
        name=f"{name}_half{half}",
    )(table, blocks, *pieces, *rest)


def shift(value, axis, up):
    count = lax.axis_size(axis)
    pairs = [(i, (i + 1) % count) for i in range(count)]
    if not up:
        pairs = [(target, source) for source, target in pairs]
    return lax.ppermute(value, axis, pairs)


def halves_kernel(blocks, moved):
    columns, faces, width, depth = blocks.shape
    part_rows = width // 2
    group = 4 * width
    row = lax.broadcasted_iota(jnp.int32, (group, group), 0)
    column = lax.broadcasted_iota(jnp.int32, (group, group), 1)
    place = (row // width) * part_rows + row % part_rows
    place = place + ((row // part_rows) % 2) * (group // 2)
    mover = jnp.where(place == column, 1.0, 0.0).astype(jnp.bfloat16)

    def turn(n, carry):
        for face in range(faces):
            for first in range(0, depth, group):
                result = jnp.dot(
                    blocks[n, face, :, first : first + group],
                    mover,
                    preferred_element_type=jnp.float32,
                ).astype(jnp.bfloat16)
                at = first // 2
                moved[n, face, :, at : at + group // 2] = result[:, : group // 2]
                at += depth // 2
                moved[n, face, :, at : at + group // 2] = result[:, group // 2 :]
        return carry

    lax.fori_loop(0, columns, turn, 0)


def halves_of_rows(blocks):
    return pl.pallas_call(
        halves_kernel,
        in_specs=[VMEM],
        out_specs=VMEM,
        out_shape=jax.ShapeDtypeStruct(blocks.shape, blocks.dtype),
        compiler_params=pltpu.CompilerParams(vmem_limit_bytes=VMEM_LIMIT),
        name="halves_of_rows",
    )(blocks)


def local(start_vector, trace_blocks, neighbour):
    columns, around, faces, width, lanes = start_vector.shape
    start = start_vector.reshape(columns, faces, width, lanes)
    blocks = halves_of_rows(trace_blocks.reshape(columns, faces, width, -1))
    codes = neighbour.reshape(faces, -1)
    table = (((codes // faces) % 3) * (columns + 2) + codes // (3 * faces)) * faces + codes % faces
    every = tuple(range(columns))
    current = list(pack(start))
    basis = None
    latest = current[0]
    lows = [shift(current[h], "azim", True) for h in range(HALVES)]
    highs = [shift(current[h], "azim", False) for h in range(HALVES)]
    waiting = None
    for index in range(STEPS):
        previous = tuple(current)
        for h in range(HALVES):
            pieces = (current[h], lows[h], highs[h])
            to_low, to_high = edges(*pieces, latest)
            stream = (shift(to_high, "stream", True), shift(to_low, "stream", False))
            middle = part(h, table, blocks, pieces, (to_low, to_high))
            if waiting is not None:
                held, _ = lax.optimization_barrier((current[waiting], middle))
                highs[waiting] = shift(held, "azim", False)
            after = middle
            if h == 1 and index > 0:
                basis, after = unpack(index - 1, every, *previous, basis, middle)
            current[h] = latest = part(h, table, blocks, pieces, (*stream, middle, after))
            waiting = None
            if index < STEPS - 1:
                lows[h] = shift(current[h], "azim", True)
                waiting = h
    basis, _ = unpack(STEPS - 1, every, *current, basis, None)
    return basis.reshape(STEPS, columns, around, faces, width, lanes)


def solution(mesh):
    return jax.shard_map(
        local,
        mesh=mesh,
        in_specs=(
            P("stream", "azim", None, None, None),
            P("stream", "azim", None, None, None),
            P("azim", None, None),
        ),
        out_specs=P(None, "stream", "azim", None, None, None),
        check_vma=False,
    )
```

```python
import functools

import jax
import jax.numpy as jnp
from jax import lax
from jax.experimental import pallas as pl
from jax.experimental.pallas import tpu as pltpu
from jax.sharding import PartitionSpec as P

STEPS = 4
HALVES = 2
APART_FIRST = (False, False)
APART_LAST = (False, True)
WEIGHT = 100
VMEM_LIMIT = 4 * 1024 * 1024
VMEM = pl.BlockSpec(memory_space=pltpu.VMEM)
ANY = pl.BlockSpec(memory_space=pl.ANY)


def low_lanes(shape):
    return lax.broadcasted_iota(jnp.int32, shape, len(shape) - 1) < shape[-1] // 2


def swap_lanes(value):
    return pltpu.roll(value, value.shape[-1] // 2, len(value.shape) - 1)


def pack_kernel(start_ref, first_ref, second_ref):
    columns, faces, width, lanes = start_ref.shape
    for column in range(columns):
        for face in range(faces):
            value = start_ref[column, face].astype(jnp.float32)
            top = value[: width // 2]
            bottom = swap_lanes(value[width // 2 :])
            low = low_lanes(top.shape)
            first_ref[column, face] = jnp.where(low, top, bottom).astype(jnp.bfloat16)
            second_ref[column, face] = jnp.where(low, bottom, top).astype(jnp.bfloat16)


def pack(start):
    columns, faces, width, lanes = start.shape
    half = jax.ShapeDtypeStruct((columns, faces, width // 2, lanes), jnp.bfloat16)
    return pl.pallas_call(
        pack_kernel,
        in_specs=[VMEM],
        out_specs=[VMEM] * 2,
        out_shape=[half, half],
        compiler_params=pltpu.CompilerParams(vmem_limit_bytes=VMEM_LIMIT),
        name="pack",
    )(start)


def unpack_kernel(index, chosen, skipped, first_ref, second_ref, *refs):
    basis_ref, done_ref, buffer, sems = refs[-4:]
    done_ref[...] = jnp.zeros_like(done_ref)
    faces, rows = first_ref.shape[1:3]
    copies = []
    for n, column in enumerate(chosen):
        for face in range(faces):
            first = first_ref[column, face].astype(jnp.float32)
            second = second_ref[column - skipped, face].astype(jnp.float32)
            low = low_lanes(first.shape)
            buffer[n, face, :rows] = jnp.where(low, first, second).astype(jnp.bfloat16)
            bottom = swap_lanes(jnp.where(low, second, first))
            buffer[n, face, rows:] = bottom.astype(jnp.bfloat16)
        copies.append(
            pltpu.make_async_copy(buffer.at[n], basis_ref.at[index, column], sems.at[n])
        )
        copies[-1].start()
    for copy in copies:
        copy.wait()


def unpack(index, chosen, first, second, basis, after):
    columns, faces, rows, lanes = first.shape
    size = len(chosen)
    skipped = 0 if second.shape[0] == columns else chosen[0]
    extra = [value for value in (basis, after) if value is not None]
    return pl.pallas_call(
        functools.partial(unpack_kernel, index, chosen, skipped),
        in_specs=[VMEM] * 2 + [ANY] * len(extra),
        out_specs=[ANY, VMEM],
        out_shape=[
            jax.ShapeDtypeStruct((STEPS, columns, faces, 2 * rows, lanes), jnp.bfloat16),
            jax.ShapeDtypeStruct((8, lanes), jnp.float32),
        ],
        scratch_shapes=[
            pltpu.VMEM((size, faces, 2 * rows, lanes), jnp.bfloat16),
            pltpu.SemaphoreType.DMA((size,)),
        ],
        input_output_aliases={} if basis is None else {2: 0},
        compiler_params=pltpu.CompilerParams(vmem_limit_bytes=VMEM_LIMIT),
        name="unpack",
    )(first, second, *extra)


def edges(own, low_az, high_az, after):
    *trio, _ = lax.optimization_barrier((low_az, own, high_az, after))
    return jnp.stack([part[0] for part in trio]), jnp.stack([part[-1] for part in trio])


def neighbours_of(value, apart):
    if apart:
        parts = (jnp.stack([value[0], value[-1]]), value[1:-1])
    else:
        parts = (value,)
    return [(part, shift(part, "azim", True), shift(part, "azim", False)) for part in parts]


def joined(value, outer, inner, after):
    outer, inner, _ = lax.optimization_barrier((outer, inner, after))
    return (
        value,
        *(jnp.concatenate([outer[n][:1], inner[n], outer[n][1:]]) for n in (1, 2)),
    )


def part_kernel(half, *refs):
    table, blocks, own, low_az, high_az = refs[:5]
    following, window = refs[-2:]
    edge = len(refs) > 9
    faces, width, depth = blocks.shape[1:]
    columns = own.shape[0]
    span = columns + 2
    rows, lanes = window.shape[1:]
    view = window.reshape(3, span, faces, rows, lanes)

    def enter(column, carry):
        for azim, source in enumerate((low_az, own, high_az)):
            for face in range(faces):
                view[azim, column + 1, face] = source[column, face]
        return carry

    lax.fori_loop(0, columns, enter, 0)
    if edge:
        low_st, high_st, before = refs[5:8]

        def enter_stream(face, carry):
            for azim in range(3):
                view[azim, 0, face] = low_st[azim, face]
                view[azim, span - 1, face] = high_st[azim, face]
            for column in range(columns - 2):
                following[column + 1, face] = before[column, face]
            return carry

        lax.fori_loop(0, faces, enter_stream, 0)
    neighbours = table.shape[1]
    low = low_lanes((rows, lanes))

    def turn(n, carry):
        column = n * (columns - 1) if edge else n + 1
        slot = column if edge else n
        for face in range(faces):
            gathered = jnp.concatenate(
                [window[table[face, k] + column * faces] for k in range(neighbours)], axis=0
            )
            block = blocks[column, face]
            stacked = jnp.concatenate([block[:, : depth // 2], block[:, depth // 2 :]], axis=0)
            product = jnp.dot(stacked, gathered, preferred_element_type=jnp.float32)
            top, bottom = product[:width], product[width:]
            if half == 0:
                here = jnp.where(low, top[:rows], bottom[rows:])
                there = jnp.where(low, top[rows:], bottom[:rows])
            else:
                here = jnp.where(low, bottom[rows:], top[:rows])
                there = jnp.where(low, bottom[:rows], top[rows:])
            following[slot, face] = (here + swap_lanes(there)).astype(jnp.bfloat16)
        return carry

    lax.fori_loop(0, 2 if edge else columns - 2, turn, 0)


def part(half, table, blocks, pieces, rest):
    columns, faces, width, depth = blocks.shape
    rows, lanes = pieces[0].shape[2:]
    edge = len(rest) > 2
    name = "edge" if edge else "inner"
    done, kept = (2, columns) if edge else (columns - 2, columns - 2)
    in_specs = [pl.BlockSpec(memory_space=pltpu.SMEM)] + [VMEM] * 4
    in_specs += [VMEM] * 3 + [ANY] if edge else [ANY] * 2
    return pl.pallas_call(
        functools.partial(part_kernel, half),
        in_specs=in_specs,
        out_specs=VMEM,
        out_shape=jax.ShapeDtypeStruct((kept, faces, rows, lanes), jnp.bfloat16),
        scratch_shapes=[pltpu.VMEM((3 * (columns + 2) * faces, rows, lanes), jnp.bfloat16)],
        cost_estimate=pl.CostEstimate(
            flops=WEIGHT * 2 * done * faces * width * depth * lanes,
            bytes_accessed=WEIGHT * 2 * done * faces * width * depth,
            transcendentals=0,
        ),
        compiler_params=pltpu.CompilerParams(vmem_limit_bytes=VMEM_LIMIT),
        name=f"{name}_half{half}",
    )(table, blocks, *pieces, *rest)


def shift(value, axis, up):
    count = lax.axis_size(axis)
    pairs = [(i, (i + 1) % count) for i in range(count)]
    if not up:
        pairs = [(target, source) for source, target in pairs]
    return lax.ppermute(value, axis, pairs)


def halves_kernel(blocks, moved):
    columns, faces, width, depth = blocks.shape
    part_rows = width // 2
    group = 4 * width
    row = lax.broadcasted_iota(jnp.int32, (group, group), 0)
    column = lax.broadcasted_iota(jnp.int32, (group, group), 1)
    place = (row // width) * part_rows + row % part_rows
    place = place + ((row // part_rows) % 2) * (group // 2)
    mover = jnp.where(place == column, 1.0, 0.0).astype(jnp.bfloat16)

    def turn(n, carry):
        for face in range(faces):
            for first in range(0, depth, group):
                result = jnp.dot(
                    blocks[n, face, :, first : first + group],
                    mover,
                    preferred_element_type=jnp.float32,
                ).astype(jnp.bfloat16)
                at = first // 2
                moved[n, face, :, at : at + group // 2] = result[:, : group // 2]
                at += depth // 2
                moved[n, face, :, at : at + group // 2] = result[:, group // 2 :]
        return carry

    lax.fori_loop(0, columns, turn, 0)


def halves_of_rows(blocks):
    return pl.pallas_call(
        halves_kernel,
        in_specs=[VMEM],
        out_specs=VMEM,
        out_shape=jax.ShapeDtypeStruct(blocks.shape, blocks.dtype),
        compiler_params=pltpu.CompilerParams(vmem_limit_bytes=VMEM_LIMIT),
        name="halves_of_rows",
    )(blocks)


def local(start_vector, trace_blocks, neighbour):
    columns, around, faces, width, lanes = start_vector.shape
    start = start_vector.reshape(columns, faces, width, lanes)
    blocks = halves_of_rows(trace_blocks.reshape(columns, faces, width, -1))
    codes = neighbour.reshape(faces, -1)
    table = (((codes // faces) % 3) * (columns + 2) + codes // (3 * faces)) * faces + codes % faces
    table = pltpu.with_memory_space_constraint(table, pltpu.SMEM)
    every = tuple(range(columns))
    current = list(pack(start))
    basis = None
    latest = current[0]
    around_z = [neighbours_of(current[h], APART_FIRST[h]) for h in range(HALVES)]
    for index in range(STEPS):
        previous = tuple(current)
        for h in range(HALVES):
            parts = around_z[h]
            apart = len(parts) > 1
            to_low, to_high = edges(*parts[0], middle if apart and h else latest)
            pieces = joined(current[h], *parts, latest if h else to_high) if apart else parts[0]
            stream = (shift(to_high, "stream", True), shift(to_low, "stream", False))
            middle = part(h, table, blocks, pieces, (to_low, to_high))
            after = middle
            if h == 1 and index > 0:
                basis, after = unpack(index - 1, every, *previous, basis, middle)
            current[h] = latest = part(h, table, blocks, pieces, (*stream, middle, after))
            if index < STEPS - 1:
                around_z[h] = neighbours_of(current[h], index == STEPS - 2 and APART_LAST[h])
    basis, _ = unpack(STEPS - 1, every, *current, basis, None)
    return basis.reshape(STEPS, columns, around, faces, width, lanes)


def solution(mesh):
    return jax.shard_map(
        local,
        mesh=mesh,
        in_specs=(
            P("stream", "azim", None, None, None),
            P("stream", "azim", None, None, None),
            P("azim", None, None),
        ),
        out_specs=P(None, "stream", "azim", None, None, None),
        check_vma=False,
    )
```

```python
import functools

import jax
import jax.numpy as jnp
from jax import lax
from jax.experimental import pallas as pl
from jax.experimental.pallas import tpu as pltpu
from jax.sharding import PartitionSpec as P

STEPS = 4
HALVES = 2
WEIGHT = 100
VMEM_LIMIT = 4 * 1024 * 1024
VMEM = pl.BlockSpec(memory_space=pltpu.VMEM)
ANY = pl.BlockSpec(memory_space=pl.ANY)


def low_lanes(shape):
    return lax.broadcasted_iota(jnp.int32, shape, len(shape) - 1) < shape[-1] // 2


def swap_lanes(value):
    return pltpu.roll(value, value.shape[-1] // 2, len(value.shape) - 1)


def pack_kernel(start_ref, first_ref, second_ref):
    columns, faces, width, lanes = start_ref.shape
    for column in range(columns):
        for face in range(faces):
            value = start_ref[column, face].astype(jnp.float32)
            top = value[: width // 2]
            bottom = swap_lanes(value[width // 2 :])
            low = low_lanes(top.shape)
            first_ref[column, face] = jnp.where(low, top, bottom).astype(jnp.bfloat16)
            second_ref[column, face] = jnp.where(low, bottom, top).astype(jnp.bfloat16)


def pack(start):
    columns, faces, width, lanes = start.shape
    half = jax.ShapeDtypeStruct((columns, faces, width // 2, lanes), jnp.bfloat16)
    return pl.pallas_call(
        pack_kernel,
        in_specs=[VMEM],
        out_specs=[VMEM] * 2,
        out_shape=[half, half],
        compiler_params=pltpu.CompilerParams(vmem_limit_bytes=VMEM_LIMIT),
        name="pack",
    )(start)


def unpack_kernel(index, chosen, skipped, first_ref, second_ref, *refs):
    basis_ref, done_ref, buffer, sems = refs[-4:]
    done_ref[...] = jnp.zeros_like(done_ref)
    faces, rows = first_ref.shape[1:3]
    copies = []
    for n, column in enumerate(chosen):
        for face in range(faces):
            first = first_ref[column, face].astype(jnp.float32)
            second = second_ref[column - skipped, face].astype(jnp.float32)
            low = low_lanes(first.shape)
            buffer[n, face, :rows] = jnp.where(low, first, second).astype(jnp.bfloat16)
            bottom = swap_lanes(jnp.where(low, second, first))
            buffer[n, face, rows:] = bottom.astype(jnp.bfloat16)
        copies.append(
            pltpu.make_async_copy(buffer.at[n], basis_ref.at[index, column], sems.at[n])
        )
        copies[-1].start()
    for copy in copies:
        copy.wait()


def unpack(index, chosen, first, second, basis, after):
    columns, faces, rows, lanes = first.shape
    size = len(chosen)
    skipped = 0 if second.shape[0] == columns else chosen[0]
    extra = [value for value in (basis, after) if value is not None]
    return pl.pallas_call(
        functools.partial(unpack_kernel, index, chosen, skipped),
        in_specs=[VMEM] * 2 + [ANY] * len(extra),
        out_specs=[ANY, VMEM],
        out_shape=[
            jax.ShapeDtypeStruct((STEPS, columns, faces, 2 * rows, lanes), jnp.bfloat16),
            jax.ShapeDtypeStruct((8, lanes), jnp.float32),
        ],
        scratch_shapes=[
            pltpu.VMEM((size, faces, 2 * rows, lanes), jnp.bfloat16),
            pltpu.SemaphoreType.DMA((size,)),
        ],
        input_output_aliases={} if basis is None else {2: 0},
        compiler_params=pltpu.CompilerParams(vmem_limit_bytes=VMEM_LIMIT),
        name="unpack",
    )(first, second, *extra)


def held(values, *after):
    return lax.optimization_barrier((tuple(values), after))[0]


def edges(values, *after):
    values = held(values, *after)
    return jnp.stack([value[0] for value in values]), jnp.stack([value[-1] for value in values])


def part_kernel(half, *refs):
    table_ref, blocks, own, low_az, high_az = refs[:5]
    following, window, index, sem = refs[-4:]
    edge = len(refs) > 13
    faces, width, depth = blocks.shape[1:]
    columns = own.shape[0]
    span = columns + 2
    rows, lanes = window.shape[1:]
    view = window.reshape(3, span, faces, rows, lanes)
    indexing = pltpu.make_async_copy(table_ref, index, sem)
    indexing.start()

    def enter(column, carry):
        for azim, source in enumerate((low_az, own, high_az)):
            for face in range(faces):
                view[azim, column + 1, face] = source[column, face]
        return carry

    lax.fori_loop(0, columns, enter, 0)
    if edge:
        low_st, high_st, low_rest, high_rest, before = refs[5:10]

        def enter_stream(face, carry):
            for azim in range(2):
                view[azim, 0, face] = low_st[azim, face]
                view[azim, span - 1, face] = high_st[azim, face]
            view[2, 0, face] = low_rest[0, face]
            view[2, span - 1, face] = high_rest[0, face]
            for column in range(columns - 2):
                following[column + 1, face] = before[column, face]
            return carry

        lax.fori_loop(0, faces, enter_stream, 0)
    indexing.wait()
    neighbours = index.shape[1]
    low = low_lanes((rows, lanes))

    def turn(n, carry):
        column = n * (columns - 1) if edge else n + 1
        slot = column if edge else n
        for face in range(faces):
            gathered = jnp.concatenate(
                [window[index[face, k] + column * faces] for k in range(neighbours)], axis=0
            )
            block = blocks[column, face]
            stacked = jnp.concatenate([block[:, : depth // 2], block[:, depth // 2 :]], axis=0)
            product = jnp.dot(stacked, gathered, preferred_element_type=jnp.float32)
            top, bottom = product[:width], product[width:]
            if half == 0:
                here = jnp.where(low, top[:rows], bottom[rows:])
                there = jnp.where(low, top[rows:], bottom[:rows])
            else:
                here = jnp.where(low, bottom[rows:], top[:rows])
                there = jnp.where(low, bottom[:rows], top[rows:])
            following[slot, face] = (here + swap_lanes(there)).astype(jnp.bfloat16)
        return carry

    lax.fori_loop(0, 2 if edge else columns - 2, turn, 0)


def part(half, table, blocks, pieces, rest):
    columns, faces, width, depth = blocks.shape
    rows, lanes = pieces[0].shape[2:]
    edge = len(rest) > 4
    name = "edge" if edge else "inner"
    done, kept = (2, columns) if edge else (columns - 2, columns - 2)
    in_specs = [ANY] + [VMEM] * 4 + ([VMEM] * 5 + [ANY] if edge else [ANY] * 4)
    return pl.pallas_call(
        functools.partial(part_kernel, half),
        in_specs=in_specs,
        out_specs=VMEM,
        out_shape=jax.ShapeDtypeStruct((kept, faces, rows, lanes), jnp.bfloat16),
        scratch_shapes=[
            pltpu.VMEM((3 * (columns + 2) * faces, rows, lanes), jnp.bfloat16),
            pltpu.SMEM(table.shape, jnp.int32),
            pltpu.SemaphoreType.DMA,
        ],
        cost_estimate=pl.CostEstimate(
            flops=WEIGHT * 2 * done * faces * width * depth * lanes,
            bytes_accessed=WEIGHT * 2 * done * faces * width * depth,
            transcendentals=0,
        ),
        compiler_params=pltpu.CompilerParams(vmem_limit_bytes=VMEM_LIMIT),
        name=f"{name}_half{half}",
    )(table, blocks, *pieces, *rest)


def shift(value, axis, up):
    count = lax.axis_size(axis)
    pairs = [(i, (i + 1) % count) for i in range(count)]
    if not up:
        pairs = [(target, source) for source, target in pairs]
    return lax.ppermute(value, axis, pairs)


def halves_kernel(blocks, moved):
    columns, faces, width, depth = blocks.shape
    part_rows = width // 2
    group = 4 * width
    row = lax.broadcasted_iota(jnp.int32, (group, group), 0)
    column = lax.broadcasted_iota(jnp.int32, (group, group), 1)
    place = (row // width) * part_rows + row % part_rows
    place = place + ((row // part_rows) % 2) * (group // 2)
    mover = jnp.where(place == column, 1.0, 0.0).astype(jnp.bfloat16)

    def turn(n, carry):
        for face in range(faces):
            for first in range(0, depth, group):
                result = jnp.dot(
                    blocks[n, face, :, first : first + group],
                    mover,
                    preferred_element_type=jnp.float32,
                ).astype(jnp.bfloat16)
                at = first // 2
                moved[n, face, :, at : at + group // 2] = result[:, : group // 2]
                at += depth // 2
                moved[n, face, :, at : at + group // 2] = result[:, group // 2 :]
        return carry

    lax.fori_loop(0, columns, turn, 0)


def halves_of_rows(blocks):
    return pl.pallas_call(
        halves_kernel,
        in_specs=[VMEM],
        out_specs=VMEM,
        out_shape=jax.ShapeDtypeStruct(blocks.shape, blocks.dtype),
        compiler_params=pltpu.CompilerParams(vmem_limit_bytes=VMEM_LIMIT),
        name="halves_of_rows",
    )(blocks)


def local(start_vector, trace_blocks, neighbour):
    columns, around, faces, width, lanes = start_vector.shape
    start = start_vector.reshape(columns, faces, width, lanes)
    blocks = halves_of_rows(trace_blocks.reshape(columns, faces, width, -1))
    codes = neighbour.reshape(faces, -1)
    table = (((codes // faces) % 3) * (columns + 2) + codes // (3 * faces)) * faces + codes % faces
    every = tuple(range(columns))
    current = list(pack(start))
    basis = None
    latest = current[0]
    lows = [shift(current[h], "azim", True) for h in range(HALVES)]
    highs = [shift(current[h], "azim", False) for h in range(HALVES)]
    for index in range(STEPS):
        previous = tuple(current)
        for h in range(HALVES):
            pieces = (current[h], lows[h], highs[h])
            to_low, to_high = edges((lows[h], current[h]), latest)
            low_st = shift(to_high, "stream", True)
            high_st = shift(to_low, "stream", False)
            rest_low, rest_high = edges((highs[h],), low_st, high_st)
            stream = (
                low_st,
                high_st,
                shift(rest_high, "stream", True),
                shift(rest_low, "stream", False),
            )
            sent = (to_low, to_high, rest_low, rest_high)
            after = middle = part(h, table, blocks, pieces, sent)
            if h == 0 and index > 0:
                basis, after = unpack(index - 1, every, *previous, basis, middle)
            current[h] = latest = part(h, table, blocks, pieces, (*stream, middle, after))
            if index < STEPS - 1:
                lows[h] = shift(current[h], "azim", True)
                highs[h] = shift(current[h], "azim", False)
    basis, _ = unpack(STEPS - 1, every, *current, basis, None)
    return basis.reshape(STEPS, columns, around, faces, width, lanes)


def solution(mesh):
    return jax.shard_map(
        local,
        mesh=mesh,
        in_specs=(
            P("stream", "azim", None, None, None),
            P("stream", "azim", None, None, None),
            P("azim", None, None),
        ),
        out_specs=P(None, "stream", "azim", None, None, None),
        check_vma=False,
    )
```

```python
import functools

import jax
import jax.numpy as jnp
from jax import lax
from jax.experimental import pallas as pl
from jax.experimental.pallas import tpu as pltpu
from jax.sharding import PartitionSpec as P

STEPS = 4
HALVES = 2
WEIGHT = 100
VMEM_LIMIT = 4 * 1024 * 1024
VMEM = pl.BlockSpec(memory_space=pltpu.VMEM)
ANY = pl.BlockSpec(memory_space=pl.ANY)


def low_lanes(shape):
    return lax.broadcasted_iota(jnp.int32, shape, len(shape) - 1) < shape[-1] // 2


def swap_lanes(value):
    return pltpu.roll(value, value.shape[-1] // 2, len(value.shape) - 1)


def pack_kernel(start_ref, first_ref, second_ref):
    columns, faces, width, lanes = start_ref.shape
    for column in range(columns):
        for face in range(faces):
            value = start_ref[column, face].astype(jnp.float32)
            top = value[: width // 2]
            bottom = swap_lanes(value[width // 2 :])
            low = low_lanes(top.shape)
            first_ref[column, face] = jnp.where(low, top, bottom).astype(jnp.bfloat16)
            second_ref[column, face] = jnp.where(low, bottom, top).astype(jnp.bfloat16)


def pack(start):
    columns, faces, width, lanes = start.shape
    half = jax.ShapeDtypeStruct((columns, faces, width // 2, lanes), jnp.bfloat16)
    return pl.pallas_call(
        pack_kernel,
        in_specs=[VMEM],
        out_specs=[VMEM] * 2,
        out_shape=[half, half],
        compiler_params=pltpu.CompilerParams(vmem_limit_bytes=VMEM_LIMIT),
        name="pack",
    )(start)


def unpack_kernel(index, chosen, skipped, first_ref, second_ref, *refs):
    basis_ref, done_ref, buffer, sems = refs[-4:]
    done_ref[...] = jnp.zeros_like(done_ref)
    faces, rows = first_ref.shape[1:3]
    copies = []
    for n, column in enumerate(chosen):
        for face in range(faces):
            first = first_ref[column, face].astype(jnp.float32)
            second = second_ref[column - skipped, face].astype(jnp.float32)
            low = low_lanes(first.shape)
            buffer[n, face, :rows] = jnp.where(low, first, second).astype(jnp.bfloat16)
            bottom = swap_lanes(jnp.where(low, second, first))
            buffer[n, face, rows:] = bottom.astype(jnp.bfloat16)
        copies.append(
            pltpu.make_async_copy(buffer.at[n], basis_ref.at[index, column], sems.at[n])
        )
        copies[-1].start()
    for copy in copies:
        copy.wait()


def unpack(index, chosen, first, second, basis, after):
    columns, faces, rows, lanes = first.shape
    size = len(chosen)
    skipped = 0 if second.shape[0] == columns else chosen[0]
    extra = [value for value in (basis, after) if value is not None]
    return pl.pallas_call(
        functools.partial(unpack_kernel, index, chosen, skipped),
        in_specs=[VMEM] * 2 + [ANY] * len(extra),
        out_specs=[ANY, VMEM],
        out_shape=[
            jax.ShapeDtypeStruct((STEPS, columns, faces, 2 * rows, lanes), jnp.bfloat16),
            jax.ShapeDtypeStruct((8, lanes), jnp.float32),
        ],
        scratch_shapes=[
            pltpu.VMEM((size, faces, 2 * rows, lanes), jnp.bfloat16),
            pltpu.SemaphoreType.DMA((size,)),
        ],
        input_output_aliases={} if basis is None else {2: 0},
        compiler_params=pltpu.CompilerParams(vmem_limit_bytes=VMEM_LIMIT),
        name="unpack",
    )(first, second, *extra)


def edges(own, low_az, high_az, after):
    *trio, _ = lax.optimization_barrier((low_az, own, high_az, after))
    return jnp.stack([part[0] for part in trio]), jnp.stack([part[-1] for part in trio])


def from_neighbours(value):
    return value, shift(value, "azim", True), shift(value, "azim", False)


def joined(value, outer, inner, after):
    outer, inner, _ = lax.optimization_barrier((outer, inner, after))
    return (
        value,
        *(jnp.concatenate([outer[n][:1], inner[n], outer[n][1:]]) for n in (1, 2)),
    )


def part_kernel(half, *refs):
    table_ref, blocks, own, low_az, high_az = refs[:5]
    following, window, index, sem = refs[-4:]
    edge = len(refs) > 11
    faces, width, depth = blocks.shape[1:]
    columns = own.shape[0]
    span = columns + 2
    rows, lanes = window.shape[1:]
    view = window.reshape(3, span, faces, rows, lanes)
    indexing = pltpu.make_async_copy(table_ref, index, sem)
    indexing.start()

    def enter(column, carry):
        for azim, source in enumerate((low_az, own, high_az)):
            for face in range(faces):
                view[azim, column + 1, face] = source[column, face]
        return carry

    lax.fori_loop(0, columns, enter, 0)
    if edge:
        low_st, high_st, before = refs[5:8]

        def enter_stream(face, carry):
            for azim in range(3):
                view[azim, 0, face] = low_st[azim, face]
                view[azim, span - 1, face] = high_st[azim, face]
            for column in range(columns - 2):
                following[column + 1, face] = before[column, face]
            return carry

        lax.fori_loop(0, faces, enter_stream, 0)
    indexing.wait()
    neighbours = index.shape[1]
    low = low_lanes((rows, lanes))

    def turn(n, carry):
        column = n * (columns - 1) if edge else n + 1
        slot = column if edge else n
        for face in range(faces):
            gathered = jnp.concatenate(
                [window[index[face, k] + column * faces] for k in range(neighbours)], axis=0
            )
            block = blocks[column, face]
            stacked = jnp.concatenate([block[:, : depth // 2], block[:, depth // 2 :]], axis=0)
            product = jnp.dot(stacked, gathered, preferred_element_type=jnp.float32)
            top, bottom = product[:width], product[width:]
            if half == 0:
                here = jnp.where(low, top[:rows], bottom[rows:])
                there = jnp.where(low, top[rows:], bottom[:rows])
            else:
                here = jnp.where(low, bottom[rows:], top[:rows])
                there = jnp.where(low, bottom[:rows], top[rows:])
            following[slot, face] = (here + swap_lanes(there)).astype(jnp.bfloat16)
        return carry

    lax.fori_loop(0, 2 if edge else columns - 2, turn, 0)


def part(half, table, blocks, pieces, rest):
    columns, faces, width, depth = blocks.shape
    rows, lanes = pieces[0].shape[2:]
    edge = len(rest) > 2
    name = "edge" if edge else "inner"
    done, kept = (2, columns) if edge else (columns - 2, columns - 2)
    in_specs = [ANY] + [VMEM] * 4
    in_specs += [VMEM] * 3 + [ANY] if edge else [ANY] * 2
    return pl.pallas_call(
        functools.partial(part_kernel, half),
        in_specs=in_specs,
        out_specs=VMEM,
        out_shape=jax.ShapeDtypeStruct((kept, faces, rows, lanes), jnp.bfloat16),
        scratch_shapes=[
            pltpu.VMEM((3 * (columns + 2) * faces, rows, lanes), jnp.bfloat16),
            pltpu.SMEM(table.shape, jnp.int32),
            pltpu.SemaphoreType.DMA,
        ],
        cost_estimate=pl.CostEstimate(
            flops=WEIGHT * 2 * done * faces * width * depth * lanes,
            bytes_accessed=WEIGHT * 2 * done * faces * width * depth,
            transcendentals=0,
        ),
        compiler_params=pltpu.CompilerParams(vmem_limit_bytes=VMEM_LIMIT),
        name=f"{name}_half{half}",
    )(table, blocks, *pieces, *rest)


def shift(value, axis, up):
    count = lax.axis_size(axis)
    pairs = [(i, (i + 1) % count) for i in range(count)]
    if not up:
        pairs = [(target, source) for source, target in pairs]
    return lax.ppermute(value, axis, pairs)


def halves_kernel(blocks, moved):
    columns, faces, width, depth = blocks.shape
    part_rows = width // 2
    group = 4 * width
    row = lax.broadcasted_iota(jnp.int32, (group, group), 0)
    column = lax.broadcasted_iota(jnp.int32, (group, group), 1)
    place = (row // width) * part_rows + row % part_rows
    place = place + ((row // part_rows) % 2) * (group // 2)
    mover = jnp.where(place == column, 1.0, 0.0).astype(jnp.bfloat16)

    def turn(n, carry):
        for face in range(faces):
            for first in range(0, depth, group):
                result = jnp.dot(
                    blocks[n, face, :, first : first + group],
                    mover,
                    preferred_element_type=jnp.float32,
                ).astype(jnp.bfloat16)
                at = first // 2
                moved[n, face, :, at : at + group // 2] = result[:, : group // 2]
                at += depth // 2
                moved[n, face, :, at : at + group // 2] = result[:, group // 2 :]
        return carry

    lax.fori_loop(0, columns, turn, 0)


def halves_of_rows(blocks):
    return pl.pallas_call(
        halves_kernel,
        in_specs=[VMEM],
        out_specs=VMEM,
        out_shape=jax.ShapeDtypeStruct(blocks.shape, blocks.dtype),
        compiler_params=pltpu.CompilerParams(vmem_limit_bytes=VMEM_LIMIT),
        name="halves_of_rows",
    )(blocks)


def local(start_vector, trace_blocks, neighbour):
    columns, around, faces, width, lanes = start_vector.shape
    start = start_vector.reshape(columns, faces, width, lanes)
    blocks = halves_of_rows(trace_blocks.reshape(columns, faces, width, -1))
    codes = neighbour.reshape(faces, -1)
    table = (((codes // faces) % 3) * (columns + 2) + codes // (3 * faces)) * faces + codes % faces
    every = tuple(range(columns))
    current = list(pack(start))
    basis = None
    latest = current[0]
    pieces = [from_neighbours(value) for value in current]
    outer = None
    for index in range(STEPS):
        previous = tuple(current)
        for h in range(HALVES):
            if outer is None or h < HALVES - 1:
                to_low, to_high = edges(*pieces[h], latest)
            else:
                own_inner, _ = lax.optimization_barrier((current[h][1:-1], middle))
                inner = from_neighbours(own_inner)
                to_low, to_high = edges(*outer, middle)
                pieces[h] = joined(current[h], outer, inner, latest)
            stream = (shift(to_high, "stream", True), shift(to_low, "stream", False))
            middle = part(h, table, blocks, pieces[h], (to_low, to_high))
            after = middle
            if h == 0 and index > 0:
                basis, after = unpack(index - 1, every, *previous, basis, middle)
            current[h] = latest = part(h, table, blocks, pieces[h], (*stream, middle, after))
            if index == STEPS - 2 and h == HALVES - 1:
                outer = from_neighbours(jnp.stack([current[h][0], current[h][-1]]))
            elif index < STEPS - 1:
                pieces[h] = from_neighbours(current[h])
    basis, _ = unpack(STEPS - 1, every, *current, basis, None)
    return basis.reshape(STEPS, columns, around, faces, width, lanes)


def solution(mesh):
    return jax.shard_map(
        local,
        mesh=mesh,
        in_specs=(
            P("stream", "azim", None, None, None),
            P("stream", "azim", None, None, None),
            P("azim", None, None),
        ),
        out_specs=P(None, "stream", "azim", None, None, None),
        check_vma=False,
    )
```

```python
import functools

import jax
import jax.numpy as jnp
from jax import lax
from jax.experimental import pallas as pl
from jax.experimental.pallas import tpu as pltpu
from jax.sharding import PartitionSpec as P

STEPS = 4
HALVES = 2
WEIGHT = 100
VMEM_LIMIT = 4 * 1024 * 1024
VMEM = pl.BlockSpec(memory_space=pltpu.VMEM)
ANY = pl.BlockSpec(memory_space=pl.ANY)


def low_lanes(shape):
    return lax.broadcasted_iota(jnp.int32, shape, len(shape) - 1) < shape[-1] // 2


def swap_lanes(value):
    return pltpu.roll(value, value.shape[-1] // 2, len(value.shape) - 1)


def pack_kernel(start_ref, first_ref, second_ref):
    columns, faces, width, lanes = start_ref.shape
    for column in range(columns):
        for face in range(faces):
            value = start_ref[column, face].astype(jnp.float32)
            top = value[: width // 2]
            bottom = swap_lanes(value[width // 2 :])
            low = low_lanes(top.shape)
            first_ref[column, face] = jnp.where(low, top, bottom).astype(jnp.bfloat16)
            second_ref[column, face] = jnp.where(low, bottom, top).astype(jnp.bfloat16)


def pack(start):
    columns, faces, width, lanes = start.shape
    half = jax.ShapeDtypeStruct((columns, faces, width // 2, lanes), jnp.bfloat16)
    return pl.pallas_call(
        pack_kernel,
        in_specs=[VMEM],
        out_specs=[VMEM] * 2,
        out_shape=[half, half],
        compiler_params=pltpu.CompilerParams(vmem_limit_bytes=VMEM_LIMIT),
        name="pack",
    )(start)


def unpack_kernel(index, chosen, skipped, first_ref, second_ref, *refs):
    basis_ref, done_ref, buffer, sems = refs[-4:]
    done_ref[...] = jnp.zeros_like(done_ref)
    faces, rows = first_ref.shape[1:3]
    copies = []
    for n, column in enumerate(chosen):
        for face in range(faces):
            first = first_ref[column, face].astype(jnp.float32)
            second = second_ref[column - skipped, face].astype(jnp.float32)
            low = low_lanes(first.shape)
            buffer[n, face, :rows] = jnp.where(low, first, second).astype(jnp.bfloat16)
            bottom = swap_lanes(jnp.where(low, second, first))
            buffer[n, face, rows:] = bottom.astype(jnp.bfloat16)
        copies.append(
            pltpu.make_async_copy(buffer.at[n], basis_ref.at[index, column], sems.at[n])
        )
        copies[-1].start()
    for copy in copies:
        copy.wait()


def unpack(index, chosen, first, second, basis, after):
    columns, faces, rows, lanes = first.shape
    size = len(chosen)
    skipped = 0 if second.shape[0] == columns else chosen[0]
    extra = [value for value in (basis, after) if value is not None]
    return pl.pallas_call(
        functools.partial(unpack_kernel, index, chosen, skipped),
        in_specs=[VMEM] * 2 + [ANY] * len(extra),
        out_specs=[ANY, VMEM],
        out_shape=[
            jax.ShapeDtypeStruct((STEPS, columns, faces, 2 * rows, lanes), jnp.bfloat16),
            jax.ShapeDtypeStruct((8, lanes), jnp.float32),
        ],
        scratch_shapes=[
            pltpu.VMEM((size, faces, 2 * rows, lanes), jnp.bfloat16),
            pltpu.SemaphoreType.DMA((size,)),
        ],
        input_output_aliases={} if basis is None else {2: 0},
        compiler_params=pltpu.CompilerParams(vmem_limit_bytes=VMEM_LIMIT),
        name="unpack",
    )(first, second, *extra)


def edges(own, low_az, high_az, after):
    *trio, _ = lax.optimization_barrier((low_az, own, high_az, after))
    return jnp.stack([part[0] for part in trio]), jnp.stack([part[-1] for part in trio])


def from_neighbours(value):
    return value, shift(value, "azim", True), shift(value, "azim", False)


def joined(value, outer, inner, after):
    outer, inner, _ = lax.optimization_barrier((outer, inner, after))
    return (
        value,
        *(jnp.concatenate([outer[n][:1], inner[n], outer[n][1:]]) for n in (1, 2)),
    )


def part_kernel(half, *refs):
    table_ref, blocks, own, low_az, high_az = refs[:5]
    following, window, index, sem = refs[-4:]
    edge = len(refs) > 11
    faces, width, depth = blocks.shape[1:]
    columns = own.shape[0]
    span = columns + 2
    rows, lanes = window.shape[1:]
    view = window.reshape(3, span, faces, rows, lanes)
    indexing = pltpu.make_async_copy(table_ref, index, sem)
    indexing.start()

    def enter(column, carry):
        for azim, source in enumerate((low_az, own, high_az)):
            for face in range(faces):
                view[azim, column + 1, face] = source[column, face]
        return carry

    lax.fori_loop(0, columns, enter, 0)
    if edge:
        high_st, low_st, before = refs[5:8]

        def enter_stream(face, carry):
            for azim in range(3):
                view[azim, 0, face] = low_st[azim, face]
                view[azim, span - 1, face] = high_st[azim, face]
            for column in range(columns - 2):
                following[column + 1, face] = before[column, face]
            return carry

        lax.fori_loop(0, faces, enter_stream, 0)
    indexing.wait()
    neighbours = index.shape[1]
    low = low_lanes((rows, lanes))

    def turn(n, carry):
        column = n * (columns - 1) if edge else n + 1
        slot = column if edge else n
        for face in range(faces):
            gathered = jnp.concatenate(
                [window[index[face, k] + column * faces] for k in range(neighbours)], axis=0
            )
            block = blocks[column, face]
            stacked = jnp.concatenate([block[:, : depth // 2], block[:, depth // 2 :]], axis=0)
            product = jnp.dot(stacked, gathered, preferred_element_type=jnp.float32)
            top, bottom = product[:width], product[width:]
            if half == 0:
                here = jnp.where(low, top[:rows], bottom[rows:])
                there = jnp.where(low, top[rows:], bottom[:rows])
            else:
                here = jnp.where(low, bottom[rows:], top[:rows])
                there = jnp.where(low, bottom[:rows], top[rows:])
            following[slot, face] = (here + swap_lanes(there)).astype(jnp.bfloat16)
        return carry

    lax.fori_loop(0, 2 if edge else columns - 2, turn, 0)


def part(half, table, blocks, pieces, rest):
    columns, faces, width, depth = blocks.shape
    rows, lanes = pieces[0].shape[2:]
    edge = len(rest) > 2
    name = "edge" if edge else "inner"
    done, kept = (2, columns) if edge else (columns - 2, columns - 2)
    in_specs = [ANY] + [VMEM] * 4
    in_specs += [VMEM] * 3 + [ANY] if edge else [ANY] * 2
    return pl.pallas_call(
        functools.partial(part_kernel, half),
        in_specs=in_specs,
        out_specs=VMEM,
        out_shape=jax.ShapeDtypeStruct((kept, faces, rows, lanes), jnp.bfloat16),
        scratch_shapes=[
            pltpu.VMEM((3 * (columns + 2) * faces, rows, lanes), jnp.bfloat16),
            pltpu.SMEM(table.shape, jnp.int32),
            pltpu.SemaphoreType.DMA,
        ],
        cost_estimate=pl.CostEstimate(
            flops=WEIGHT * 2 * done * faces * width * depth * lanes,
            bytes_accessed=WEIGHT * 2 * done * faces * width * depth,
            transcendentals=0,
        ),
        compiler_params=pltpu.CompilerParams(vmem_limit_bytes=VMEM_LIMIT),
        name=f"{name}_half{half}",
    )(table, blocks, *pieces, *rest)


def shift(value, axis, up):
    count = lax.axis_size(axis)
    pairs = [(i, (i + 1) % count) for i in range(count)]
    if not up:
        pairs = [(target, source) for source, target in pairs]
    return lax.ppermute(value, axis, pairs)


def halves_kernel(blocks, moved):
    columns, faces, width, depth = blocks.shape
    part_rows = width // 2
    group = 4 * width
    row = lax.broadcasted_iota(jnp.int32, (group, group), 0)
    column = lax.broadcasted_iota(jnp.int32, (group, group), 1)
    place = (row // width) * part_rows + row % part_rows
    place = place + ((row // part_rows) % 2) * (group // 2)
    mover = jnp.where(place == column, 1.0, 0.0).astype(jnp.bfloat16)

    def turn(n, carry):
        for face in range(faces):
            for first in range(0, depth, group):
                result = jnp.dot(
                    blocks[n, face, :, first : first + group],
                    mover,
                    preferred_element_type=jnp.float32,
                ).astype(jnp.bfloat16)
                at = first // 2
                moved[n, face, :, at : at + group // 2] = result[:, : group // 2]
                at += depth // 2
                moved[n, face, :, at : at + group // 2] = result[:, group // 2 :]
        return carry

    lax.fori_loop(0, columns, turn, 0)


def halves_of_rows(blocks):
    return pl.pallas_call(
        halves_kernel,
        in_specs=[VMEM],
        out_specs=VMEM,
        out_shape=jax.ShapeDtypeStruct(blocks.shape, blocks.dtype),
        compiler_params=pltpu.CompilerParams(vmem_limit_bytes=VMEM_LIMIT),
        name="halves_of_rows",
    )(blocks)


def local(start_vector, trace_blocks, neighbour):
    columns, around, faces, width, lanes = start_vector.shape
    start = start_vector.reshape(columns, faces, width, lanes)
    blocks = halves_of_rows(trace_blocks.reshape(columns, faces, width, -1))
    codes = neighbour.reshape(faces, -1)
    table = (((codes // faces) % 3) * (columns + 2) + codes // (3 * faces)) * faces + codes % faces
    every = tuple(range(columns))
    current = list(pack(start))
    basis = None
    latest = current[0]
    pieces = [from_neighbours(value) for value in current]
    outer = None
    for index in range(STEPS):
        previous = tuple(current)
        for h in range(HALVES):
            if outer is None or h < HALVES - 1:
                to_low, to_high = edges(*pieces[h], latest)
            else:
                own_inner, _ = lax.optimization_barrier((current[h][1:-1], middle))
                inner = from_neighbours(own_inner)
                to_low, to_high = edges(*outer, middle)
                pieces[h] = joined(current[h], outer, inner, latest)
            stream = (shift(to_low, "stream", False), shift(to_high, "stream", True))
            middle = part(h, table, blocks, pieces[h], (to_high, to_low))
            after = middle
            if h == 0 and index > 0:
                basis, after = unpack(index - 1, every, *previous, basis, middle)
            current[h] = latest = part(h, table, blocks, pieces[h], (*stream, middle, after))
            if index == STEPS - 2 and h == HALVES - 1:
                outer = from_neighbours(jnp.stack([current[h][0], current[h][-1]]))
            elif index < STEPS - 1:
                pieces[h] = from_neighbours(current[h])
    basis, _ = unpack(STEPS - 1, every, *current, basis, None)
    return basis.reshape(STEPS, columns, around, faces, width, lanes)


def solution(mesh):
    return jax.shard_map(
        local,
        mesh=mesh,
        in_specs=(
            P("stream", "azim", None, None, None),
            P("stream", "azim", None, None, None),
            P("azim", None, None),
        ),
        out_specs=P(None, "stream", "azim", None, None, None),
        check_vma=False,
    )
```

```python
import functools

import jax
import jax.numpy as jnp
from jax import lax
from jax.experimental import pallas as pl
from jax.experimental.pallas import tpu as pltpu
from jax.sharding import PartitionSpec as P

STEPS = 4
HALVES = 2
WEIGHT = 100
VMEM_LIMIT = 4 * 1024 * 1024
VMEM = pl.BlockSpec(memory_space=pltpu.VMEM)
ANY = pl.BlockSpec(memory_space=pl.ANY)


def low_lanes(shape):
    return lax.broadcasted_iota(jnp.int32, shape, len(shape) - 1) < shape[-1] // 2


def swap_lanes(value):
    return pltpu.roll(value, value.shape[-1] // 2, len(value.shape) - 1)


def pack_kernel(start_ref, first_ref, second_ref):
    columns, faces, width, lanes = start_ref.shape
    for column in range(columns):
        for face in range(faces):
            value = start_ref[column, face].astype(jnp.float32)
            top = value[: width // 2]
            bottom = swap_lanes(value[width // 2 :])
            low = low_lanes(top.shape)
            first_ref[column, face] = jnp.where(low, top, bottom).astype(jnp.bfloat16)
            second_ref[column, face] = jnp.where(low, bottom, top).astype(jnp.bfloat16)


def pack(start):
    columns, faces, width, lanes = start.shape
    half = jax.ShapeDtypeStruct((columns, faces, width // 2, lanes), jnp.bfloat16)
    return pl.pallas_call(
        pack_kernel,
        in_specs=[VMEM],
        out_specs=[VMEM] * 2,
        out_shape=[half, half],
        compiler_params=pltpu.CompilerParams(vmem_limit_bytes=VMEM_LIMIT),
        name="pack",
    )(start)


def unpack_kernel(index, chosen, skipped, first_ref, second_ref, *refs):
    basis_ref, done_ref, buffer, sems = refs[-4:]
    done_ref[...] = jnp.zeros_like(done_ref)
    faces, rows = first_ref.shape[1:3]
    copies = []
    for n, column in enumerate(chosen):
        for face in range(faces):
            first = first_ref[column, face].astype(jnp.float32)
            second = second_ref[column - skipped, face].astype(jnp.float32)
            low = low_lanes(first.shape)
            buffer[n, face, :rows] = jnp.where(low, first, second).astype(jnp.bfloat16)
            bottom = swap_lanes(jnp.where(low, second, first))
            buffer[n, face, rows:] = bottom.astype(jnp.bfloat16)
        copies.append(
            pltpu.make_async_copy(buffer.at[n], basis_ref.at[index, column], sems.at[n])
        )
        copies[-1].start()
    for copy in copies:
        copy.wait()


def unpack(index, chosen, first, second, basis, after):
    columns, faces, rows, lanes = first.shape
    size = len(chosen)
    skipped = 0 if second.shape[0] == columns else chosen[0]
    extra = [value for value in (basis, after) if value is not None]
    return pl.pallas_call(
        functools.partial(unpack_kernel, index, chosen, skipped),
        in_specs=[VMEM] * 2 + [ANY] * len(extra),
        out_specs=[ANY, VMEM],
        out_shape=[
            jax.ShapeDtypeStruct((STEPS, columns, faces, 2 * rows, lanes), jnp.bfloat16),
            jax.ShapeDtypeStruct((8, lanes), jnp.float32),
        ],
        scratch_shapes=[
            pltpu.VMEM((size, faces, 2 * rows, lanes), jnp.bfloat16),
            pltpu.SemaphoreType.DMA((size,)),
        ],
        input_output_aliases={} if basis is None else {2: 0},
        compiler_params=pltpu.CompilerParams(vmem_limit_bytes=VMEM_LIMIT),
        name="unpack",
    )(first, second, *extra)


def edges(own, low_az, high_az, after):
    *trio, _ = lax.optimization_barrier((low_az, own, high_az, after))
    return jnp.stack([part[0] for part in trio]), jnp.stack([part[-1] for part in trio])


def from_neighbours(value, half):
    return value, *(shift(value, "azim", up) for up in (half == 0, half > 0))


def joined(value, outer, inner, after):
    outer, inner, _ = lax.optimization_barrier((outer, inner, after))
    return (
        value,
        *(jnp.concatenate([outer[n][:1], inner[n], outer[n][1:]]) for n in (1, 2)),
    )


def part_kernel(half, *refs):
    table_ref, blocks, own, low_az, high_az = refs[:5]
    following, window, index, sem = refs[-4:]
    edge = len(refs) > 11
    faces, width, depth = blocks.shape[1:]
    columns = own.shape[0]
    span = columns + 2
    rows, lanes = window.shape[1:]
    view = window.reshape(3, span, faces, rows, lanes)
    indexing = pltpu.make_async_copy(table_ref, index, sem)
    indexing.start()

    def enter(column, carry):
        for azim, source in enumerate((low_az, own, high_az)):
            for face in range(faces):
                view[azim, column + 1, face] = source[column, face]
        return carry

    lax.fori_loop(0, columns, enter, 0)
    if edge:
        high_st, low_st, before = refs[5:8]

        def enter_stream(face, carry):
            for azim in range(3):
                view[azim, 0, face] = low_st[azim, face]
                view[azim, span - 1, face] = high_st[azim, face]
            for column in range(columns - 2):
                following[column + 1, face] = before[column, face]
            return carry

        lax.fori_loop(0, faces, enter_stream, 0)
    indexing.wait()
    neighbours = index.shape[1]
    low = low_lanes((rows, lanes))

    def turn(n, carry):
        column = n * (columns - 1) if edge else n + 1
        slot = column if edge else n
        for face in range(faces):
            gathered = jnp.concatenate(
                [window[index[face, k] + column * faces] for k in range(neighbours)], axis=0
            )
            block = blocks[column, face]
            stacked = jnp.concatenate([block[:, : depth // 2], block[:, depth // 2 :]], axis=0)
            product = jnp.dot(stacked, gathered, preferred_element_type=jnp.float32)
            top, bottom = product[:width], product[width:]
            if half == 0:
                here = jnp.where(low, top[:rows], bottom[rows:])
                there = jnp.where(low, top[rows:], bottom[:rows])
            else:
                here = jnp.where(low, bottom[rows:], top[:rows])
                there = jnp.where(low, bottom[:rows], top[rows:])
            following[slot, face] = (here + swap_lanes(there)).astype(jnp.bfloat16)
        return carry

    lax.fori_loop(0, 2 if edge else columns - 2, turn, 0)


def part(half, table, blocks, pieces, rest):
    columns, faces, width, depth = blocks.shape
    rows, lanes = pieces[0].shape[2:]
    edge = len(rest) > 2
    name = "edge" if edge else "inner"
    done, kept = (2, columns) if edge else (columns - 2, columns - 2)
    in_specs = [ANY] + [VMEM] * 4
    in_specs += [VMEM] * 3 + [ANY] if edge else [ANY] * 2
    return pl.pallas_call(
        functools.partial(part_kernel, half),
        in_specs=in_specs,
        out_specs=VMEM,
        out_shape=jax.ShapeDtypeStruct((kept, faces, rows, lanes), jnp.bfloat16),
        scratch_shapes=[
            pltpu.VMEM((3 * (columns + 2) * faces, rows, lanes), jnp.bfloat16),
            pltpu.SMEM(table.shape, jnp.int32),
            pltpu.SemaphoreType.DMA,
        ],
        cost_estimate=pl.CostEstimate(
            flops=WEIGHT * 2 * done * faces * width * depth * lanes,
            bytes_accessed=WEIGHT * 2 * done * faces * width * depth,
            transcendentals=0,
        ),
        compiler_params=pltpu.CompilerParams(vmem_limit_bytes=VMEM_LIMIT),
        name=f"{name}_half{half}",
    )(table, blocks, *pieces, *rest)


def shift(value, axis, up):
    count = lax.axis_size(axis)
    pairs = [(i, (i + 1) % count) for i in range(count)]
    if not up:
        pairs = [(target, source) for source, target in pairs]
    return lax.ppermute(value, axis, pairs)


def halves_kernel(blocks, moved):
    columns, faces, width, depth = blocks.shape
    part_rows = width // 2
    group = 4 * width
    row = lax.broadcasted_iota(jnp.int32, (group, group), 0)
    column = lax.broadcasted_iota(jnp.int32, (group, group), 1)
    place = (row // width) * part_rows + row % part_rows
    place = place + ((row // part_rows) % 2) * (group // 2)
    mover = jnp.where(place == column, 1.0, 0.0).astype(jnp.bfloat16)

    def turn(n, carry):
        for face in range(faces):
            for first in range(0, depth, group):
                result = jnp.dot(
                    blocks[n, face, :, first : first + group],
                    mover,
                    preferred_element_type=jnp.float32,
                ).astype(jnp.bfloat16)
                at = first // 2
                moved[n, face, :, at : at + group // 2] = result[:, : group // 2]
                at += depth // 2
                moved[n, face, :, at : at + group // 2] = result[:, group // 2 :]
        return carry

    lax.fori_loop(0, columns, turn, 0)


def halves_of_rows(blocks):
    return pl.pallas_call(
        halves_kernel,
        in_specs=[VMEM],
        out_specs=VMEM,
        out_shape=jax.ShapeDtypeStruct(blocks.shape, blocks.dtype),
        compiler_params=pltpu.CompilerParams(vmem_limit_bytes=VMEM_LIMIT),
        name="halves_of_rows",
    )(blocks)


def local(start_vector, trace_blocks, neighbour):
    columns, around, faces, width, lanes = start_vector.shape
    start = start_vector.reshape(columns, faces, width, lanes)
    blocks = halves_of_rows(trace_blocks.reshape(columns, faces, width, -1))
    codes = neighbour.reshape(faces, -1)
    around_shift = (codes // faces) % 3
    tables = [
        (place * (columns + 2) + codes // (3 * faces)) * faces + codes % faces
        for place in (around_shift, 2 - around_shift)
    ]
    every = tuple(range(columns))
    current = list(pack(start))
    basis = None
    latest = current[0]
    pieces = [from_neighbours(value, h) for h, value in enumerate(current)]
    outer = None
    for index in range(STEPS):
        previous = tuple(current)
        for h in range(HALVES):
            if outer is None or h < HALVES - 1:
                to_low, to_high = edges(*pieces[h], latest)
            else:
                own_inner, _ = lax.optimization_barrier((current[h][1:-1], middle))
                inner = from_neighbours(own_inner, h)
                to_low, to_high = edges(*outer, middle)
                pieces[h] = joined(current[h], outer, inner, latest)
            stream = (shift(to_low, "stream", False), shift(to_high, "stream", True))
            middle = part(h, tables[h], blocks, pieces[h], (to_high, to_low))
            after = middle
            if h == 0 and index > 0:
                basis, after = unpack(index - 1, every, *previous, basis, middle)
            current[h] = latest = part(h, tables[h], blocks, pieces[h], (*stream, middle, after))
            if index == STEPS - 2 and h == HALVES - 1:
                outer = from_neighbours(jnp.stack([current[h][0], current[h][-1]]), h)
            elif index < STEPS - 1:
                pieces[h] = from_neighbours(current[h], h)
    basis, _ = unpack(STEPS - 1, every, *current, basis, None)
    return basis.reshape(STEPS, columns, around, faces, width, lanes)


def solution(mesh):
    return jax.shard_map(
        local,
        mesh=mesh,
        in_specs=(
            P("stream", "azim", None, None, None),
            P("stream", "azim", None, None, None),
            P("azim", None, None),
        ),
        out_specs=P(None, "stream", "azim", None, None, None),
        check_vma=False,
    )
```

```python
import functools

import jax
import jax.numpy as jnp
from jax import lax
from jax.experimental import pallas as pl
from jax.experimental.pallas import tpu as pltpu
from jax.sharding import PartitionSpec as P

STEPS = 4
HALVES = 2
WEIGHT = 100
VMEM_LIMIT = 4 * 1024 * 1024
VMEM = pl.BlockSpec(memory_space=pltpu.VMEM)
ANY = pl.BlockSpec(memory_space=pl.ANY)


def low_lanes(shape):
    return lax.broadcasted_iota(jnp.int32, shape, len(shape) - 1) < shape[-1] // 2


def swap_lanes(value):
    return pltpu.roll(value, value.shape[-1] // 2, len(value.shape) - 1)


def pack_kernel(start_ref, first_ref, second_ref):
    columns, faces, width, lanes = start_ref.shape
    for column in range(columns):
        for face in range(faces):
            value = start_ref[column, face].astype(jnp.float32)
            top = value[: width // 2]
            bottom = swap_lanes(value[width // 2 :])
            low = low_lanes(top.shape)
            first_ref[column, face] = jnp.where(low, top, bottom).astype(jnp.bfloat16)
            second_ref[column, face] = jnp.where(low, bottom, top).astype(jnp.bfloat16)


def pack(start):
    columns, faces, width, lanes = start.shape
    half = jax.ShapeDtypeStruct((columns, faces, width // 2, lanes), jnp.bfloat16)
    return pl.pallas_call(
        pack_kernel,
        in_specs=[VMEM],
        out_specs=[VMEM] * 2,
        out_shape=[half, half],
        compiler_params=pltpu.CompilerParams(vmem_limit_bytes=VMEM_LIMIT),
        name="pack",
    )(start)


def unpack_kernel(index, chosen, skipped, first_ref, second_ref, *refs):
    basis_ref, done_ref, buffer, sems = refs[-4:]
    done_ref[...] = jnp.zeros_like(done_ref)
    faces, rows = first_ref.shape[1:3]
    copies = []
    for n, column in enumerate(chosen):
        for face in range(faces):
            first = first_ref[column, face].astype(jnp.float32)
            second = second_ref[column - skipped, face].astype(jnp.float32)
            low = low_lanes(first.shape)
            buffer[n, face, :rows] = jnp.where(low, first, second).astype(jnp.bfloat16)
            bottom = swap_lanes(jnp.where(low, second, first))
            buffer[n, face, rows:] = bottom.astype(jnp.bfloat16)
        copies.append(
            pltpu.make_async_copy(buffer.at[n], basis_ref.at[index, column], sems.at[n])
        )
        copies[-1].start()
    for copy in copies:
        copy.wait()


def unpack(index, chosen, first, second, basis, after):
    columns, faces, rows, lanes = first.shape
    size = len(chosen)
    skipped = 0 if second.shape[0] == columns else chosen[0]
    extra = [value for value in (basis, after) if value is not None]
    return pl.pallas_call(
        functools.partial(unpack_kernel, index, chosen, skipped),
        in_specs=[VMEM] * 2 + [ANY] * len(extra),
        out_specs=[ANY, VMEM],
        out_shape=[
            jax.ShapeDtypeStruct((STEPS, columns, faces, 2 * rows, lanes), jnp.bfloat16),
            jax.ShapeDtypeStruct((8, lanes), jnp.float32),
        ],
        scratch_shapes=[
            pltpu.VMEM((size, faces, 2 * rows, lanes), jnp.bfloat16),
            pltpu.SemaphoreType.DMA((size,)),
        ],
        input_output_aliases={} if basis is None else {2: 0},
        compiler_params=pltpu.CompilerParams(vmem_limit_bytes=VMEM_LIMIT),
        name="unpack",
    )(first, second, *extra)


def edges(own, high_az, low_az, after):
    *trio, _ = lax.optimization_barrier((high_az, own, low_az, after))
    return jnp.stack([part[0] for part in trio]), jnp.stack([part[-1] for part in trio])


def from_neighbours(value):
    return value, shift(value, "azim", False), shift(value, "azim", True)


def joined(value, outer, inner, after):
    outer, inner, _ = lax.optimization_barrier((outer, inner, after))
    return (
        value,
        *(jnp.concatenate([outer[n][:1], inner[n], outer[n][1:]]) for n in (1, 2)),
    )


def part_kernel(half, *refs):
    table_ref, blocks, own, high_az, low_az = refs[:5]
    following, window, index, sem = refs[-4:]
    edge = len(refs) > 11
    faces, width, depth = blocks.shape[1:]
    columns = own.shape[0]
    span = columns + 2
    rows, lanes = window.shape[1:]
    view = window.reshape(3, span, faces, rows, lanes)
    indexing = pltpu.make_async_copy(table_ref, index, sem)
    indexing.start()

    def enter(column, carry):
        for azim, source in enumerate((high_az, own, low_az)):
            for face in range(faces):
                view[azim, column + 1, face] = source[column, face]
        return carry

    lax.fori_loop(0, columns, enter, 0)
    if edge:
        high_st, low_st, before = refs[5:8]

        def enter_stream(face, carry):
            for azim in range(3):
                view[azim, 0, face] = low_st[azim, face]
                view[azim, span - 1, face] = high_st[azim, face]
            for column in range(columns - 2):
                following[column + 1, face] = before[column, face]
            return carry

        lax.fori_loop(0, faces, enter_stream, 0)
    indexing.wait()
    neighbours = index.shape[1]
    low = low_lanes((rows, lanes))

    def turn(n, carry):
        column = n * (columns - 1) if edge else n + 1
        slot = column if edge else n
        for face in range(faces):
            gathered = jnp.concatenate(
                [window[index[face, k] + column * faces] for k in range(neighbours)], axis=0
            )
            block = blocks[column, face]
            stacked = jnp.concatenate([block[:, : depth // 2], block[:, depth // 2 :]], axis=0)
            product = jnp.dot(stacked, gathered, preferred_element_type=jnp.float32)
            top, bottom = product[:width], product[width:]
            if half == 0:
                here = jnp.where(low, top[:rows], bottom[rows:])
                there = jnp.where(low, top[rows:], bottom[:rows])
            else:
                here = jnp.where(low, bottom[rows:], top[:rows])
                there = jnp.where(low, bottom[:rows], top[rows:])
            following[slot, face] = (here + swap_lanes(there)).astype(jnp.bfloat16)
        return carry

    lax.fori_loop(0, 2 if edge else columns - 2, turn, 0)


def part(half, table, blocks, pieces, rest):
    columns, faces, width, depth = blocks.shape
    rows, lanes = pieces[0].shape[2:]
    edge = len(rest) > 2
    name = "edge" if edge else "inner"
    done, kept = (2, columns) if edge else (columns - 2, columns - 2)
    in_specs = [ANY] + [VMEM] * 4
    in_specs += [VMEM] * 3 + [ANY] if edge else [ANY] * 2
    return pl.pallas_call(
        functools.partial(part_kernel, half),
        in_specs=in_specs,
        out_specs=VMEM,
        out_shape=jax.ShapeDtypeStruct((kept, faces, rows, lanes), jnp.bfloat16),
        scratch_shapes=[
            pltpu.VMEM((3 * (columns + 2) * faces, rows, lanes), jnp.bfloat16),
            pltpu.SMEM(table.shape, jnp.int32),
            pltpu.SemaphoreType.DMA,
        ],
        cost_estimate=pl.CostEstimate(
            flops=WEIGHT * 2 * done * faces * width * depth * lanes,
            bytes_accessed=WEIGHT * 2 * done * faces * width * depth,
            transcendentals=0,
        ),
        compiler_params=pltpu.CompilerParams(vmem_limit_bytes=VMEM_LIMIT),
        name=f"{name}_half{half}",
    )(table, blocks, *pieces, *rest)


def shift(value, axis, up):
    count = lax.axis_size(axis)
    pairs = [(i, (i + 1) % count) for i in range(count)]
    if not up:
        pairs = [(target, source) for source, target in pairs]
    return lax.ppermute(value, axis, pairs)


def halves_kernel(blocks, moved):
    columns, faces, width, depth = blocks.shape
    part_rows = width // 2
    group = 4 * width
    row = lax.broadcasted_iota(jnp.int32, (group, group), 0)
    column = lax.broadcasted_iota(jnp.int32, (group, group), 1)
    place = (row // width) * part_rows + row % part_rows
    place = place + ((row // part_rows) % 2) * (group // 2)
    mover = jnp.where(place == column, 1.0, 0.0).astype(jnp.bfloat16)

    def turn(n, carry):
        for face in range(faces):
            for first in range(0, depth, group):
                result = jnp.dot(
                    blocks[n, face, :, first : first + group],
                    mover,
                    preferred_element_type=jnp.float32,
                ).astype(jnp.bfloat16)
                at = first // 2
                moved[n, face, :, at : at + group // 2] = result[:, : group // 2]
                at += depth // 2
                moved[n, face, :, at : at + group // 2] = result[:, group // 2 :]
        return carry

    lax.fori_loop(0, columns, turn, 0)


def halves_of_rows(blocks):
    return pl.pallas_call(
        halves_kernel,
        in_specs=[VMEM],
        out_specs=VMEM,
        out_shape=jax.ShapeDtypeStruct(blocks.shape, blocks.dtype),
        compiler_params=pltpu.CompilerParams(vmem_limit_bytes=VMEM_LIMIT),
        name="halves_of_rows",
    )(blocks)


def local(start_vector, trace_blocks, neighbour):
    columns, around, faces, width, lanes = start_vector.shape
    start = start_vector.reshape(columns, faces, width, lanes)
    blocks = halves_of_rows(trace_blocks.reshape(columns, faces, width, -1))
    codes = neighbour.reshape(faces, -1)
    around_shift = 2 - (codes // faces) % 3
    table = (around_shift * (columns + 2) + codes // (3 * faces)) * faces + codes % faces
    every = tuple(range(columns))
    current = list(pack(start))
    basis = None
    latest = current[0]
    pieces = [from_neighbours(value) for value in current]
    outer = None
    for index in range(STEPS):
        previous = tuple(current)
        for h in range(HALVES):
            if outer is None or h < HALVES - 1:
                to_low, to_high = edges(*pieces[h], latest)
            else:
                own_inner, _ = lax.optimization_barrier((current[h][1:-1], middle))
                inner = from_neighbours(own_inner)
                to_low, to_high = edges(*outer, middle)
                pieces[h] = joined(current[h], outer, inner, latest)
            stream = (shift(to_low, "stream", False), shift(to_high, "stream", True))
            middle = part(h, table, blocks, pieces[h], (to_high, to_low))
            after = middle
            if h == 0 and index > 0:
                basis, after = unpack(index - 1, every, *previous, basis, middle)
            current[h] = latest = part(h, table, blocks, pieces[h], (*stream, middle, after))
            if index == STEPS - 2 and h == HALVES - 1:
                outer = from_neighbours(jnp.stack([current[h][0], current[h][-1]]))
            elif index < STEPS - 1:
                pieces[h] = from_neighbours(current[h])
    basis, _ = unpack(STEPS - 1, every, *current, basis, None)
    return basis.reshape(STEPS, columns, around, faces, width, lanes)


def solution(mesh):
    return jax.shard_map(
        local,
        mesh=mesh,
        in_specs=(
            P("stream", "azim", None, None, None),
            P("stream", "azim", None, None, None),
            P("azim", None, None),
        ),
        out_specs=P(None, "stream", "azim", None, None, None),
        check_vma=False,
    )
```

```python
import functools

import jax
import jax.numpy as jnp
from jax import lax
from jax.experimental import pallas as pl
from jax.experimental.pallas import tpu as pltpu
from jax.sharding import PartitionSpec as P

STEPS = 4
HALVES = 2
WEIGHT = 100
VMEM_LIMIT = 4 * 1024 * 1024
VMEM = pl.BlockSpec(memory_space=pltpu.VMEM)
ANY = pl.BlockSpec(memory_space=pl.ANY)


def low_lanes(shape):
    return lax.broadcasted_iota(jnp.int32, shape, len(shape) - 1) < shape[-1] // 2


def swap_lanes(value):
    return pltpu.roll(value, value.shape[-1] // 2, len(value.shape) - 1)


def pack_kernel(start_ref, first_ref, second_ref):
    columns, faces, width, lanes = start_ref.shape
    for column in range(columns):
        for face in range(faces):
            value = start_ref[column, face].astype(jnp.float32)
            top = value[: width // 2]
            bottom = swap_lanes(value[width // 2 :])
            low = low_lanes(top.shape)
            first_ref[column, face] = jnp.where(low, top, bottom).astype(jnp.bfloat16)
            second_ref[column, face] = jnp.where(low, bottom, top).astype(jnp.bfloat16)


def pack(start):
    columns, faces, width, lanes = start.shape
    half = jax.ShapeDtypeStruct((columns, faces, width // 2, lanes), jnp.bfloat16)
    return pl.pallas_call(
        pack_kernel,
        in_specs=[VMEM],
        out_specs=[VMEM] * 2,
        out_shape=[half, half],
        compiler_params=pltpu.CompilerParams(vmem_limit_bytes=VMEM_LIMIT),
        name="pack",
    )(start)


def unpack_kernel(index, chosen, skipped, first_ref, second_ref, *refs):
    basis_ref, done_ref, buffer, sems = refs[-4:]
    done_ref[...] = jnp.zeros_like(done_ref)
    faces, rows = first_ref.shape[1:3]
    copies = []
    for n, column in enumerate(chosen):
        for face in range(faces):
            first = first_ref[column, face].astype(jnp.float32)
            second = second_ref[column - skipped, face].astype(jnp.float32)
            low = low_lanes(first.shape)
            buffer[n, face, :rows] = jnp.where(low, first, second).astype(jnp.bfloat16)
            bottom = swap_lanes(jnp.where(low, second, first))
            buffer[n, face, rows:] = bottom.astype(jnp.bfloat16)
        copies.append(
            pltpu.make_async_copy(buffer.at[n], basis_ref.at[index, column], sems.at[n])
        )
        copies[-1].start()
    for copy in copies:
        copy.wait()


def unpack(index, chosen, first, second, basis, after):
    columns, faces, rows, lanes = first.shape
    size = len(chosen)
    skipped = 0 if second.shape[0] == columns else chosen[0]
    extra = [value for value in (basis, after) if value is not None]
    return pl.pallas_call(
        functools.partial(unpack_kernel, index, chosen, skipped),
        in_specs=[VMEM] * 2 + [ANY] * len(extra),
        out_specs=[ANY, VMEM],
        out_shape=[
            jax.ShapeDtypeStruct((STEPS, columns, faces, 2 * rows, lanes), jnp.bfloat16),
            jax.ShapeDtypeStruct((8, lanes), jnp.float32),
        ],
        scratch_shapes=[
            pltpu.VMEM((size, faces, 2 * rows, lanes), jnp.bfloat16),
            pltpu.SemaphoreType.DMA((size,)),
        ],
        input_output_aliases={} if basis is None else {2: 0},
        compiler_params=pltpu.CompilerParams(vmem_limit_bytes=VMEM_LIMIT),
        name="unpack",
    )(first, second, *extra)


def edges(own, high_az, low_az, after):
    *trio, _ = lax.optimization_barrier((high_az, own, low_az, after))
    return jnp.stack([part[0] for part in trio]), jnp.stack([part[-1] for part in trio])


def from_neighbours(value):
    return value, shift(value, "azim", False), shift(value, "azim", True)


def joined(value, outer, inner, after):
    outer, inner, _ = lax.optimization_barrier((outer, inner, after))
    return (
        value,
        *(jnp.concatenate([outer[n][:1], inner[n], outer[n][1:]]) for n in (1, 2)),
    )


def part_kernel(half, *refs):
    table_ref, blocks, own, high_az, low_az = refs[:5]
    following, window, index, sem = refs[-4:]
    edge = len(refs) > 11
    faces, width, depth = blocks.shape[1:]
    columns = own.shape[0]
    span = columns + 2
    rows, lanes = window.shape[1:]
    view = window.reshape(3, span, faces, rows, lanes)
    indexing = pltpu.make_async_copy(table_ref, index, sem)
    indexing.start()

    def enter(column, carry):
        for azim, source in enumerate((high_az, own, low_az)):
            for face in range(faces):
                view[azim, column + 1, face] = source[column, face]
        return carry

    lax.fori_loop(0, columns, enter, 0)
    if edge:
        low_st, high_st, before = refs[5:8]

        def enter_stream(face, carry):
            for azim in range(3):
                view[azim, 0, face] = low_st[azim, face]
                view[azim, span - 1, face] = high_st[azim, face]
            for column in range(columns - 2):
                following[column + 1, face] = before[column, face]
            return carry

        lax.fori_loop(0, faces, enter_stream, 0)
    indexing.wait()
    neighbours = index.shape[1]
    low = low_lanes((rows, lanes))

    def turn(n, carry):
        column = n * (columns - 1) if edge else n + 1
        slot = column if edge else n
        for face in range(faces):
            gathered = jnp.concatenate(
                [window[index[face, k] + column * faces] for k in range(neighbours)], axis=0
            )
            block = blocks[column, face]
            stacked = jnp.concatenate([block[:, : depth // 2], block[:, depth // 2 :]], axis=0)
            product = jnp.dot(stacked, gathered, preferred_element_type=jnp.float32)
            top, bottom = product[:width], product[width:]
            if half == 0:
                here = jnp.where(low, top[:rows], bottom[rows:])
                there = jnp.where(low, top[rows:], bottom[:rows])
            else:
                here = jnp.where(low, bottom[rows:], top[:rows])
                there = jnp.where(low, bottom[:rows], top[rows:])
            following[slot, face] = (here + swap_lanes(there)).astype(jnp.bfloat16)
        return carry

    lax.fori_loop(0, 2 if edge else columns - 2, turn, 0)


def part(half, table, blocks, pieces, rest):
    columns, faces, width, depth = blocks.shape
    rows, lanes = pieces[0].shape[2:]
    edge = len(rest) > 2
    name = "edge" if edge else "inner"
    done, kept = (2, columns) if edge else (columns - 2, columns - 2)
    in_specs = [ANY] + [VMEM] * 4
    in_specs += [VMEM] * 3 + [ANY] if edge else [ANY] * 2
    return pl.pallas_call(
        functools.partial(part_kernel, half),
        in_specs=in_specs,
        out_specs=VMEM,
        out_shape=jax.ShapeDtypeStruct((kept, faces, rows, lanes), jnp.bfloat16),
        scratch_shapes=[
            pltpu.VMEM((3 * (columns + 2) * faces, rows, lanes), jnp.bfloat16),
            pltpu.SMEM(table.shape, jnp.int32),
            pltpu.SemaphoreType.DMA,
        ],
        cost_estimate=pl.CostEstimate(
            flops=WEIGHT * 2 * done * faces * width * depth * lanes,
            bytes_accessed=WEIGHT * 2 * done * faces * width * depth,
            transcendentals=0,
        ),
        compiler_params=pltpu.CompilerParams(vmem_limit_bytes=VMEM_LIMIT),
        name=f"{name}_half{half}",
    )(table, blocks, *pieces, *rest)


def shift(value, axis, up):
    count = lax.axis_size(axis)
    pairs = [(i, (i + 1) % count) for i in range(count)]
    if not up:
        pairs = [(target, source) for source, target in pairs]
    return lax.ppermute(value, axis, pairs)


def halves_kernel(blocks, moved):
    columns, faces, width, depth = blocks.shape
    part_rows = width // 2
    group = 4 * width
    row = lax.broadcasted_iota(jnp.int32, (group, group), 0)
    column = lax.broadcasted_iota(jnp.int32, (group, group), 1)
    place = (row // width) * part_rows + row % part_rows
    place = place + ((row // part_rows) % 2) * (group // 2)
    mover = jnp.where(place == column, 1.0, 0.0).astype(jnp.bfloat16)

    def turn(n, carry):
        for face in range(faces):
            for first in range(0, depth, group):
                result = jnp.dot(
                    blocks[n, face, :, first : first + group],
                    mover,
                    preferred_element_type=jnp.float32,
                ).astype(jnp.bfloat16)
                at = first // 2
                moved[n, face, :, at : at + group // 2] = result[:, : group // 2]
                at += depth // 2
                moved[n, face, :, at : at + group // 2] = result[:, group // 2 :]
        return carry

    lax.fori_loop(0, columns, turn, 0)


def halves_of_rows(blocks):
    return pl.pallas_call(
        halves_kernel,
        in_specs=[VMEM],
        out_specs=VMEM,
        out_shape=jax.ShapeDtypeStruct(blocks.shape, blocks.dtype),
        compiler_params=pltpu.CompilerParams(vmem_limit_bytes=VMEM_LIMIT),
        name="halves_of_rows",
    )(blocks)


def local(start_vector, trace_blocks, neighbour):
    columns, around, faces, width, lanes = start_vector.shape
    start = start_vector.reshape(columns, faces, width, lanes)
    blocks = halves_of_rows(trace_blocks.reshape(columns, faces, width, -1))
    codes = neighbour.reshape(faces, -1)
    around_shift = 2 - (codes // faces) % 3
    table = (around_shift * (columns + 2) + codes // (3 * faces)) * faces + codes % faces
    every = tuple(range(columns))
    current = list(pack(start))
    basis = None
    latest = current[0]
    pieces = [from_neighbours(value) for value in current]
    outer = None
    for index in range(STEPS):
        previous = tuple(current)
        for h in range(HALVES):
            if outer is None or h < HALVES - 1:
                to_low, to_high = edges(*pieces[h], latest)
            else:
                own_inner, _ = lax.optimization_barrier((current[h][1:-1], packed))
                inner = from_neighbours(own_inner)
                to_low, to_high = edges(*outer, middle)
                pieces[h] = joined(current[h], outer, inner, latest)
            packed = to_high
            stream = (shift(to_high, "stream", True), shift(to_low, "stream", False))
            middle = part(h, table, blocks, pieces[h], (to_low, to_high))
            after = middle
            if index > 0 and h == (index == STEPS - 1):
                basis, after = unpack(index - 1, every, *previous, basis, latest if h else middle)
            current[h] = latest = part(h, table, blocks, pieces[h], (*stream, middle, after))
            if index == STEPS - 2 and h == HALVES - 1:
                outer = from_neighbours(jnp.stack([current[h][0], current[h][-1]]))
            elif index < STEPS - 1:
                pieces[h] = from_neighbours(current[h])
    basis, _ = unpack(STEPS - 1, every, *current, basis, None)
    return basis.reshape(STEPS, columns, around, faces, width, lanes)


def solution(mesh):
    return jax.shard_map(
        local,
        mesh=mesh,
        in_specs=(
            P("stream", "azim", None, None, None),
            P("stream", "azim", None, None, None),
            P("azim", None, None),
        ),
        out_specs=P(None, "stream", "azim", None, None, None),
        check_vma=False,
    )
```

```python
import functools

import jax
import jax.numpy as jnp
from jax import lax
from jax.experimental import pallas as pl
from jax.experimental.pallas import tpu as pltpu
from jax.sharding import PartitionSpec as P

STEPS = 4
HALVES = 2
WEIGHT = 100
VMEM_LIMIT = 4 * 1024 * 1024
VMEM = pl.BlockSpec(memory_space=pltpu.VMEM)
ANY = pl.BlockSpec(memory_space=pl.ANY)


def low_lanes(shape):
    return lax.broadcasted_iota(jnp.int32, shape, len(shape) - 1) < shape[-1] // 2


def swap_lanes(value):
    return pltpu.roll(value, value.shape[-1] // 2, len(value.shape) - 1)


def pack_kernel(start_ref, first_ref, second_ref):
    columns, faces, width, lanes = start_ref.shape
    for column in range(columns):
        for face in range(faces):
            value = start_ref[column, face].astype(jnp.float32)
            top = value[: width // 2]
            bottom = swap_lanes(value[width // 2 :])
            low = low_lanes(top.shape)
            first_ref[column, face] = jnp.where(low, top, bottom).astype(jnp.bfloat16)
            second_ref[column, face] = jnp.where(low, bottom, top).astype(jnp.bfloat16)


def pack(start):
    columns, faces, width, lanes = start.shape
    half = jax.ShapeDtypeStruct((columns, faces, width // 2, lanes), jnp.bfloat16)
    return pl.pallas_call(
        pack_kernel,
        in_specs=[VMEM],
        out_specs=[VMEM] * 2,
        out_shape=[half, half],
        compiler_params=pltpu.CompilerParams(vmem_limit_bytes=VMEM_LIMIT),
        name="pack",
    )(start)


def unpack_kernel(index, chosen, skipped, first_ref, second_ref, *refs):
    basis_ref, done_ref, buffer, sems = refs[-4:]
    done_ref[...] = jnp.zeros_like(done_ref)
    faces, rows = first_ref.shape[1:3]
    copies = []
    for n, column in enumerate(chosen):
        for face in range(faces):
            first = first_ref[column, face].astype(jnp.float32)
            second = second_ref[column - skipped, face].astype(jnp.float32)
            low = low_lanes(first.shape)
            buffer[n, face, :rows] = jnp.where(low, first, second).astype(jnp.bfloat16)
            bottom = swap_lanes(jnp.where(low, second, first))
            buffer[n, face, rows:] = bottom.astype(jnp.bfloat16)
        copies.append(
            pltpu.make_async_copy(buffer.at[n], basis_ref.at[index, column], sems.at[n])
        )
        copies[-1].start()
    for copy in copies:
        copy.wait()


def unpack(index, chosen, first, second, basis, after):
    columns, faces, rows, lanes = first.shape
    size = len(chosen)
    skipped = 0 if second.shape[0] == columns else chosen[0]
    extra = [value for value in (basis, after) if value is not None]
    return pl.pallas_call(
        functools.partial(unpack_kernel, index, chosen, skipped),
        in_specs=[VMEM] * 2 + [ANY] * len(extra),
        out_specs=[ANY, VMEM],
        out_shape=[
            jax.ShapeDtypeStruct((STEPS, columns, faces, 2 * rows, lanes), jnp.bfloat16),
            jax.ShapeDtypeStruct((8, lanes), jnp.float32),
        ],
        scratch_shapes=[
            pltpu.VMEM((size, faces, 2 * rows, lanes), jnp.bfloat16),
            pltpu.SemaphoreType.DMA((size,)),
        ],
        input_output_aliases={} if basis is None else {2: 0},
        compiler_params=pltpu.CompilerParams(vmem_limit_bytes=VMEM_LIMIT),
        name="unpack",
    )(first, second, *extra)


def edges(own, low_az, high_az, after):
    *trio, _ = lax.optimization_barrier((low_az, own, high_az, after))
    return jnp.stack([part[0] for part in trio]), jnp.stack([part[-1] for part in trio])


def from_neighbours(value):
    return value, shift(value, "azim", True), shift(value, "azim", False)


def joined(value, outer, inner, after):
    outer, inner, _ = lax.optimization_barrier((outer, inner, after))
    return (
        value,
        *(jnp.concatenate([outer[n][:1], inner[n], outer[n][1:]]) for n in (1, 2)),
    )


def part_kernel(half, *refs):
    table_ref, blocks, own, low_az, high_az = refs[:5]
    following, window, index, sem = refs[-4:]
    edge = len(refs) > 11
    faces, width, depth = blocks.shape[1:]
    columns = own.shape[0]
    span = columns + 2
    rows, lanes = window.shape[1:]
    view = window.reshape(3, span, faces, rows, lanes)
    indexing = pltpu.make_async_copy(table_ref, index, sem)
    indexing.start()

    def enter(column, carry):
        for azim, source in enumerate((low_az, own, high_az)):
            for face in range(faces):
                view[azim, column + 1, face] = source[column, face]
        return carry

    lax.fori_loop(0, columns, enter, 0)
    if edge:
        low_st, high_st, before = refs[5:8]

        def enter_stream(face, carry):
            for azim in range(3):
                view[azim, 0, face] = low_st[azim, face]
                view[azim, span - 1, face] = high_st[azim, face]
            for column in range(columns - 2):
                following[column + 1, face] = before[column, face]
            return carry

        lax.fori_loop(0, faces, enter_stream, 0)
    indexing.wait()
    neighbours = index.shape[1]
    low = low_lanes((rows, lanes))

    def turn(n, carry):
        column = n * (columns - 1) if edge else n + 1
        slot = column if edge else n
        for face in range(faces):
            gathered = jnp.concatenate(
                [window[index[face, k] + column * faces] for k in range(neighbours)], axis=0
            )
            block = blocks[column, face]
            stacked = jnp.concatenate([block[:, : depth // 2], block[:, depth // 2 :]], axis=0)
            product = jnp.dot(stacked, gathered, preferred_element_type=jnp.float32)
            top, bottom = product[:width], product[width:]
            if half == 0:
                here = jnp.where(low, top[:rows], bottom[rows:])
                there = jnp.where(low, top[rows:], bottom[:rows])
            else:
                here = jnp.where(low, bottom[rows:], top[:rows])
                there = jnp.where(low, bottom[:rows], top[rows:])
            following[slot, face] = (here + swap_lanes(there)).astype(jnp.bfloat16)
        return carry

    lax.fori_loop(0, 2 if edge else columns - 2, turn, 0)


def part(half, table, blocks, pieces, rest):
    columns, faces, width, depth = blocks.shape
    rows, lanes = pieces[0].shape[2:]
    edge = len(rest) > 2
    name = "edge" if edge else "inner"
    done, kept = (2, columns) if edge else (columns - 2, columns - 2)
    in_specs = [ANY] + [VMEM] * 4
    in_specs += [VMEM] * 3 + [ANY] if edge else [ANY] * 2
    return pl.pallas_call(
        functools.partial(part_kernel, half),
        in_specs=in_specs,
        out_specs=VMEM,
        out_shape=jax.ShapeDtypeStruct((kept, faces, rows, lanes), jnp.bfloat16),
        scratch_shapes=[
            pltpu.VMEM((3 * (columns + 2) * faces, rows, lanes), jnp.bfloat16),
            pltpu.SMEM(table.shape, jnp.int32),
            pltpu.SemaphoreType.DMA,
        ],
        cost_estimate=pl.CostEstimate(
            flops=WEIGHT * 2 * done * faces * width * depth * lanes,
            bytes_accessed=WEIGHT * 2 * done * faces * width * depth,
            transcendentals=0,
        ),
        compiler_params=pltpu.CompilerParams(vmem_limit_bytes=VMEM_LIMIT),
        name=f"{name}_half{half}",
    )(table, blocks, *pieces, *rest)


def shift(value, axis, up):
    count = lax.axis_size(axis)
    pairs = [(i, (i + 1) % count) for i in range(count)]
    if not up:
        pairs = [(target, source) for source, target in pairs]
    return lax.ppermute(value, axis, pairs)


def halves_kernel(blocks, moved):
    columns, faces, width, depth = blocks.shape
    part_rows = width // 2
    group = 4 * width
    row = lax.broadcasted_iota(jnp.int32, (group, group), 0)
    column = lax.broadcasted_iota(jnp.int32, (group, group), 1)
    place = (row // width) * part_rows + row % part_rows
    place = place + ((row // part_rows) % 2) * (group // 2)
    mover = jnp.where(place == column, 1.0, 0.0).astype(jnp.bfloat16)

    def turn(n, carry):
        for face in range(faces):
            for first in range(0, depth, group):
                result = jnp.dot(
                    blocks[n, face, :, first : first + group],
                    mover,
                    preferred_element_type=jnp.float32,
                ).astype(jnp.bfloat16)
                at = first // 2
                moved[n, face, :, at : at + group // 2] = result[:, : group // 2]
                at += depth // 2
                moved[n, face, :, at : at + group // 2] = result[:, group // 2 :]
        return carry

    lax.fori_loop(0, columns, turn, 0)


def halves_of_rows(blocks):
    return pl.pallas_call(
        halves_kernel,
        in_specs=[VMEM],
        out_specs=VMEM,
        out_shape=jax.ShapeDtypeStruct(blocks.shape, blocks.dtype),
        compiler_params=pltpu.CompilerParams(vmem_limit_bytes=VMEM_LIMIT),
        name="halves_of_rows",
    )(blocks)


def local(start_vector, trace_blocks, neighbour):
    columns, around, faces, width, lanes = start_vector.shape
    start = start_vector.reshape(columns, faces, width, lanes)
    blocks = halves_of_rows(trace_blocks.reshape(columns, faces, width, -1))
    codes = neighbour.reshape(faces, -1)
    around_shift = (codes // faces) % 3
    table = (around_shift * (columns + 2) + codes // (3 * faces)) * faces + codes % faces
    every = tuple(range(columns))
    current = list(pack(start))
    basis = None
    latest = current[0]
    pieces = [from_neighbours(value) for value in current]
    outer = None
    for index in range(STEPS):
        previous = tuple(current)
        for h in range(HALVES):
            if outer is None or h < HALVES - 1:
                to_low, to_high = edges(*pieces[h], latest)
            else:
                own_inner, _ = lax.optimization_barrier((current[h][1:-1], middle))
                inner = from_neighbours(own_inner)
                to_low, to_high = edges(*outer, middle)
                pieces[h] = joined(current[h], outer, inner, latest)
            stream = (shift(to_high, "stream", True), shift(to_low, "stream", False))
            middle = part(h, table, blocks, pieces[h], (to_low, to_high))
            after = middle
            if index > 0 and h == (index == STEPS - 1):
                basis, after = unpack(index - 1, every, *previous, basis, latest if h else middle)
            current[h] = latest = part(h, table, blocks, pieces[h], (*stream, middle, after))
            if index == STEPS - 2 and h == HALVES - 1:
                outer = from_neighbours(jnp.stack([current[h][0], current[h][-1]]))
            elif index < STEPS - 1:
                pieces[h] = from_neighbours(current[h])
    basis, _ = unpack(STEPS - 1, every, *current, basis, None)
    return basis.reshape(STEPS, columns, around, faces, width, lanes)


def solution(mesh):
    return jax.shard_map(
        local,
        mesh=mesh,
        in_specs=(
            P("stream", "azim", None, None, None),
            P("stream", "azim", None, None, None),
            P("azim", None, None),
        ),
        out_specs=P(None, "stream", "azim", None, None, None),
        check_vma=False,
    )
```

```python
import functools

import jax
import jax.numpy as jnp
from jax import lax
from jax.experimental import pallas as pl
from jax.experimental.pallas import tpu as pltpu
from jax.sharding import PartitionSpec as P

STEPS = 4
HALVES = 2
WEIGHT = 100
VMEM_LIMIT = 4 * 1024 * 1024
VMEM = pl.BlockSpec(memory_space=pltpu.VMEM)
ANY = pl.BlockSpec(memory_space=pl.ANY)


def low_lanes(shape):
    return lax.broadcasted_iota(jnp.int32, shape, len(shape) - 1) < shape[-1] // 2


def swap_lanes(value):
    return pltpu.roll(value, value.shape[-1] // 2, len(value.shape) - 1)


def pack_kernel(start_ref, first_ref, second_ref):
    columns, faces, width, lanes = start_ref.shape
    for column in range(columns):
        for face in range(faces):
            value = start_ref[column, face].astype(jnp.float32)
            top = value[: width // 2]
            bottom = swap_lanes(value[width // 2 :])
            low = low_lanes(top.shape)
            first_ref[column, face] = jnp.where(low, top, bottom).astype(jnp.bfloat16)
            second_ref[column, face] = jnp.where(low, bottom, top).astype(jnp.bfloat16)


def pack(start):
    columns, faces, width, lanes = start.shape
    half = jax.ShapeDtypeStruct((columns, faces, width // 2, lanes), jnp.bfloat16)
    return pl.pallas_call(
        pack_kernel,
        in_specs=[VMEM],
        out_specs=[VMEM] * 2,
        out_shape=[half, half],
        compiler_params=pltpu.CompilerParams(vmem_limit_bytes=VMEM_LIMIT),
        name="pack",
    )(start)


def unpack_kernel(index, chosen, skipped, first_ref, second_ref, *refs):
    basis_ref, done_ref, buffer, sems = refs[-4:]
    done_ref[...] = jnp.zeros_like(done_ref)
    faces, rows = first_ref.shape[1:3]
    copies = []
    for n, column in enumerate(chosen):
        for face in range(faces):
            first = first_ref[column, face].astype(jnp.float32)
            second = second_ref[column - skipped, face].astype(jnp.float32)
            low = low_lanes(first.shape)
            buffer[n, face, :rows] = jnp.where(low, first, second).astype(jnp.bfloat16)
            bottom = swap_lanes(jnp.where(low, second, first))
            buffer[n, face, rows:] = bottom.astype(jnp.bfloat16)
        copies.append(
            pltpu.make_async_copy(buffer.at[n], basis_ref.at[index, column], sems.at[n])
        )
        copies[-1].start()
    for copy in copies:
        copy.wait()


def unpack(index, chosen, first, second, basis, after):
    columns, faces, rows, lanes = first.shape
    size = len(chosen)
    skipped = 0 if second.shape[0] == columns else chosen[0]
    extra = [value for value in (basis, after) if value is not None]
    return pl.pallas_call(
        functools.partial(unpack_kernel, index, chosen, skipped),
        in_specs=[VMEM] * 2 + [ANY] * len(extra),
        out_specs=[ANY, VMEM],
        out_shape=[
            jax.ShapeDtypeStruct((STEPS, columns, faces, 2 * rows, lanes), jnp.bfloat16),
            jax.ShapeDtypeStruct((8, lanes), jnp.float32),
        ],
        scratch_shapes=[
            pltpu.VMEM((size, faces, 2 * rows, lanes), jnp.bfloat16),
            pltpu.SemaphoreType.DMA((size,)),
        ],
        input_output_aliases={} if basis is None else {2: 0},
        compiler_params=pltpu.CompilerParams(vmem_limit_bytes=VMEM_LIMIT),
        name="unpack",
    )(first, second, *extra)


def edges(own, low_az, high_az, after):
    *trio, _ = lax.optimization_barrier((low_az, own, high_az, after))
    return jnp.stack([part[0] for part in trio]), jnp.stack([part[-1] for part in trio])


def from_neighbours(value, half):
    return value, *(shift(value, "azim", up) for up in (half > 0, half == 0))


def joined(value, outer, inner, after):
    outer, inner, _ = lax.optimization_barrier((outer, inner, after))
    return (
        value,
        *(jnp.concatenate([outer[n][:1], inner[n], outer[n][1:]]) for n in (1, 2)),
    )


def part_kernel(half, *refs):
    table_ref, blocks, own, low_az, high_az = refs[:5]
    following, window, index, sem = refs[-4:]
    edge = len(refs) > 11
    faces, width, depth = blocks.shape[1:]
    columns = own.shape[0]
    span = columns + 2
    rows, lanes = window.shape[1:]
    view = window.reshape(3, span, faces, rows, lanes)
    indexing = pltpu.make_async_copy(table_ref, index, sem)
    indexing.start()

    def enter(column, carry):
        for azim, source in enumerate((low_az, own, high_az)):
            for face in range(faces):
                view[azim, column + 1, face] = source[column, face]
        return carry

    lax.fori_loop(0, columns, enter, 0)
    if edge:
        low_st, high_st, before = refs[5:8]

        def enter_stream(face, carry):
            for azim in range(3):
                view[azim, 0, face] = low_st[azim, face]
                view[azim, span - 1, face] = high_st[azim, face]
            for column in range(columns - 2):
                following[column + 1, face] = before[column, face]
            return carry

        lax.fori_loop(0, faces, enter_stream, 0)
    indexing.wait()
    neighbours = index.shape[1]
    low = low_lanes((rows, lanes))

    def turn(n, carry):
        column = n * (columns - 1) if edge else n + 1
        slot = column if edge else n
        for face in range(faces):
            gathered = jnp.concatenate(
                [window[index[face, k] + column * faces] for k in range(neighbours)], axis=0
            )
            block = blocks[column, face]
            stacked = jnp.concatenate([block[:, : depth // 2], block[:, depth // 2 :]], axis=0)
            product = jnp.dot(stacked, gathered, preferred_element_type=jnp.float32)
            top, bottom = product[:width], product[width:]
            if half == 0:
                here = jnp.where(low, top[:rows], bottom[rows:])
                there = jnp.where(low, top[rows:], bottom[:rows])
            else:
                here = jnp.where(low, bottom[rows:], top[:rows])
                there = jnp.where(low, bottom[:rows], top[rows:])
            following[slot, face] = (here + swap_lanes(there)).astype(jnp.bfloat16)
        return carry

    lax.fori_loop(0, 2 if edge else columns - 2, turn, 0)


def part(half, table, blocks, pieces, rest):
    columns, faces, width, depth = blocks.shape
    rows, lanes = pieces[0].shape[2:]
    edge = len(rest) > 2
    name = "edge" if edge else "inner"
    done, kept = (2, columns) if edge else (columns - 2, columns - 2)
    in_specs = [ANY] + [VMEM] * 4
    in_specs += [VMEM] * 3 + [ANY] if edge else [ANY] * 2
    return pl.pallas_call(
        functools.partial(part_kernel, half),
        in_specs=in_specs,
        out_specs=VMEM,
        out_shape=jax.ShapeDtypeStruct((kept, faces, rows, lanes), jnp.bfloat16),
        scratch_shapes=[
            pltpu.VMEM((3 * (columns + 2) * faces, rows, lanes), jnp.bfloat16),
            pltpu.SMEM(table.shape, jnp.int32),
            pltpu.SemaphoreType.DMA,
        ],
        cost_estimate=pl.CostEstimate(
            flops=WEIGHT * 2 * done * faces * width * depth * lanes,
            bytes_accessed=WEIGHT * 2 * done * faces * width * depth,
            transcendentals=0,
        ),
        compiler_params=pltpu.CompilerParams(vmem_limit_bytes=VMEM_LIMIT),
        name=f"{name}_half{half}",
    )(table, blocks, *pieces, *rest)


def shift(value, axis, up):
    count = lax.axis_size(axis)
    pairs = [(i, (i + 1) % count) for i in range(count)]
    if not up:
        pairs = [(target, source) for source, target in pairs]
    return lax.ppermute(value, axis, pairs)


def halves_kernel(blocks, moved):
    columns, faces, width, depth = blocks.shape
    part_rows = width // 2
    group = 4 * width
    row = lax.broadcasted_iota(jnp.int32, (group, group), 0)
    column = lax.broadcasted_iota(jnp.int32, (group, group), 1)
    place = (row // width) * part_rows + row % part_rows
    place = place + ((row // part_rows) % 2) * (group // 2)
    mover = jnp.where(place == column, 1.0, 0.0).astype(jnp.bfloat16)

    def turn(n, carry):
        for face in range(faces):
            for first in range(0, depth, group):
                result = jnp.dot(
                    blocks[n, face, :, first : first + group],
                    mover,
                    preferred_element_type=jnp.float32,
                ).astype(jnp.bfloat16)
                at = first // 2
                moved[n, face, :, at : at + group // 2] = result[:, : group // 2]
                at += depth // 2
                moved[n, face, :, at : at + group // 2] = result[:, group // 2 :]
        return carry

    lax.fori_loop(0, columns, turn, 0)


def halves_of_rows(blocks):
    return pl.pallas_call(
        halves_kernel,
        in_specs=[VMEM],
        out_specs=VMEM,
        out_shape=jax.ShapeDtypeStruct(blocks.shape, blocks.dtype),
        compiler_params=pltpu.CompilerParams(vmem_limit_bytes=VMEM_LIMIT),
        name="halves_of_rows",
    )(blocks)


def local(start_vector, trace_blocks, neighbour):
    columns, around, faces, width, lanes = start_vector.shape
    start = start_vector.reshape(columns, faces, width, lanes)
    blocks = halves_of_rows(trace_blocks.reshape(columns, faces, width, -1))
    codes = neighbour.reshape(faces, -1)
    around_shift = (codes // faces) % 3
    tables = [
        (place * (columns + 2) + codes // (3 * faces)) * faces + codes % faces
        for place in (2 - around_shift, around_shift)
    ]
    every = tuple(range(columns))
    current = list(pack(start))
    basis = None
    latest = current[0]
    pieces = [from_neighbours(value, h) for h, value in enumerate(current)]
    outer = None
    for index in range(STEPS):
        previous = tuple(current)
        for h in range(HALVES):
            if outer is None or h < HALVES - 1:
                to_low, to_high = edges(*pieces[h], latest)
            else:
                own_inner, _ = lax.optimization_barrier((current[h][1:-1], middle))
                inner = from_neighbours(own_inner, h)
                to_low, to_high = edges(*outer, middle)
                pieces[h] = joined(current[h], outer, inner, latest)
            stream = (shift(to_high, "stream", True), shift(to_low, "stream", False))
            middle = part(h, tables[h], blocks, pieces[h], (to_low, to_high))
            after = middle
            if index > 0 and h == (index == STEPS - 1):
                basis, after = unpack(index - 1, every, *previous, basis, latest if h else middle)
            current[h] = latest = part(h, tables[h], blocks, pieces[h], (*stream, middle, after))
            if index == STEPS - 2 and h == HALVES - 1:
                outer = from_neighbours(jnp.stack([current[h][0], current[h][-1]]), h)
            elif index < STEPS - 1:
                pieces[h] = from_neighbours(current[h], h)
    basis, _ = unpack(STEPS - 1, every, *current, basis, None)
    return basis.reshape(STEPS, columns, around, faces, width, lanes)


def solution(mesh):
    return jax.shard_map(
        local,
        mesh=mesh,
        in_specs=(
            P("stream", "azim", None, None, None),
            P("stream", "azim", None, None, None),
            P("azim", None, None),
        ),
        out_specs=P(None, "stream", "azim", None, None, None),
        check_vma=False,
    )
```
